128 devices in a mesh: rows: 64 (over z, y, x), seq: 2 (over core).
Axes of the slice: x: 4, y: 4, z: 4, core: 2. Of those that a mesh axis runs over, the one named last changes fastest.
Arguments:
- enc_rows: bfloat16 [32768, 1408], P(('rows', 'seq')), may hold values from -6 to 6
- visible_pos: int32 [32768], P(('rows', 'seq')), may hold values from 0 to 131071, as said below
- enc_norm_gain: float32 [2, 1408], replicated, may hold values from 0.1 to 1.9
- enc_fc1: bfloat16 [1408, 6144], P(None, 'seq'), may hold values from -0.15625 to 0.15625
- enc_fc1_bias: float32 [6144], P('seq'), may hold values from -3 to 3
- enc_fc2: bfloat16 [6144, 1408], P('seq'), may hold values from -0.078125 to 0.078125
- enc_fc2_bias: float32 [1408], replicated, may hold values from -3 to 3
- handoff_weight: bfloat16 [1408, 512], replicated, may hold values from -0.15625 to 0.15625
- mask_token: float32 [512], replicated, may hold values from -4 to 4
- dec_norm_gain: float32 [2, 512], replicated, may hold values from 0.1 to 1.9
- qkv_weight: bfloat16 [512, 1536], replicated
- qkv_bias: float32 [1536], replicated, may hold values from -3 to 3
- out_weight: bfloat16 [512, 512], replicated, may hold values from -0.25 to 0.25
- out_bias: float32 [512], replicated, may hold values from -3 to 3
- dec_fc1: bfloat16 [512, 2048], replicated, may hold values from -0.25 to 0.25
- dec_fc1_bias: float32 [2048], replicated, may hold values from -3 to 3
- dec_fc2: bfloat16 [2048, 512], replicated, may hold values from -0.125 to 0.125
- dec_fc2_bias: float32 [512], replicated, may hold values from -3 to 3
Outputs:
- decoded: bfloat16 [64, 2048, 512], P('rows', 'seq')
The draws below stay inside these ranges and needn't reach their ends.
Inputs may be any that keep to these rules, and one draw needn't show every extreme that they name: `visible_pos`: all values differ. Number the devices of rows and seq together as d = rows index * 2 + seq index; decoder device d holds clips of rows index and tokens of seq index. Every decoder device's block receives at most 768 visible tokens, and one device's block receives exactly that many in every draw. The visible tokens of all blocks, in order of block and then position, are dealt out one at a time to devices 0, 1, 2, ... in turn, so no device holds more than 6 tokens of one block, and some device holds exactly 6 of one.
All inputs are finite; a program needn't handle non-finite values.
Results may differ from the reference program's by a relative error of at most 0.013.
Values may be sent and summed in bfloat16 or wider, within the bound.
No kernel may reach another device: no remote copies, remote signals or barrier semaphores. Data moves between devices by JAX's collectives and lax.ppermute only.
A program may use at most 256 MiB of HBM per device.

```python
import math
import jax
import jax.numpy as jnp
from jax import lax

ENC_D = 1408
ENC_FF = 6144
DD = 512
HEADS = 8
DEC_FF = 2048
CLIP_LEN = 2048
CLIPS_ROW = 1
VIS_DEV = 256
CLIPS = 64
TOTAL_VIS = 32768
N_SEQ = 2
DEVICES = 128


def draw_visible_pos(key, part):
    key = jax.random.fold_in(key, 11)
    span = CLIP_LEN // N_SEQ
    block = CLIPS_ROW * span
    key_b, key_w, key_p = jax.random.split(key, 3)
    busiest = jax.random.randint(key_b, (), 0, DEVICES)
    device = jnp.arange(DEVICES)
    shares = jnp.where(device == busiest, 0, jax.random.randint(key_w, (DEVICES,), 2, 5))
    remaining = TOTAL_VIS - 3 * VIS_DEV
    base = remaining * shares // jnp.sum(shares)
    leftover = remaining - jnp.sum(base)
    others = jnp.cumsum((shares > 0).astype(jnp.int32)) - 1
    extra = ((shares > 0) & (others < leftover)).astype(jnp.int32)
    counts = base + extra + jnp.where(device == busiest, 3 * VIS_DEV, 0)
    orders = jax.vmap(lambda sub: jax.random.permutation(sub, block))(jax.random.split(key_p, DEVICES))
    chosen = orders < counts[:, None]
    place = jnp.arange(block)
    clip = (device // N_SEQ)[:, None] * CLIPS_ROW + place[None, :] // span
    token = (device % N_SEQ)[:, None] * span + place[None, :] % span
    value = (clip * CLIP_LEN + token).reshape(-1).astype(jnp.int32)
    flat = chosen.reshape(-1)
    index = jnp.cumsum(flat.astype(jnp.int32)) - 1
    listed = jnp.zeros((TOTAL_VIS,), jnp.int32).at[jnp.where(flat, index, TOTAL_VIS)].set(value, mode='drop')
    return jnp.transpose(listed.reshape(VIS_DEV, DEVICES)).reshape(-1)


def draw_qkv_weight(key, part):
    key = jax.random.fold_in(key, 23)
    key_q, key_k, key_v = jax.random.split(key, 3)
    query = jax.random.normal(key_q, (DD, DD), jnp.float32) / math.sqrt(DD)
    keys = jax.random.normal(key_k, (DD, DD), jnp.float32) / math.sqrt(DD)
    values = jax.random.normal(key_v, (DD, DD), jnp.float32) / math.sqrt(DD)
    return jnp.concatenate([query, keys, values], axis=1).astype(jnp.bfloat16)


def steps_of(own_key, extent, cuts, low, top_value):
    level = 1.0
    for dim, blocks in cuts:
        draws = jax.random.uniform(jax.random.fold_in(jax.random.fold_in(own_key, 6), dim), (blocks,), jnp.float32, low / len(cuts), top_value / len(cuts))
        level = level * jnp.repeat(jnp.exp(draws), extent[dim] // blocks).reshape((-1,) + (1,) * (len(extent) - 1 - dim))
    return level


def normal_values(rng, shape, scale, bound, pieces=(), kind=jnp.bfloat16):
    loudness = steps_of(rng, shape, pieces, -0.22, 0.18) if pieces else 1.0
    result = jax.random.normal(rng, shape, jnp.float32) * scale * loudness
    return jnp.minimum(jnp.maximum(result, -bound), bound).astype(kind)


def setup_inputs(seed: int = 0) -> dict:
    key_list = jax.random.split(jax.random.key(seed), 19)
    return {
        "enc_rows": normal_values(key_list[0], (TOTAL_VIS, ENC_D), 1.0, 6.0, ((0, 128),)),
        "visible_pos": draw_visible_pos(jax.random.fold_in(key_list[18], 71), 0),
        "enc_norm_gain": jnp.clip(1.0 + 0.18 * jax.random.normal(key_list[2], (2, ENC_D), jnp.float32), 0.1, 1.9),
        "enc_fc1": normal_values(key_list[3], (ENC_D, ENC_FF), ENC_D ** -0.5, 0.15625, ((1, 2),)),
        "enc_fc1_bias": normal_values(key_list[4], (ENC_FF,), 0.5, 3.0, ((0, 2),), jnp.float32),
        "enc_fc2": normal_values(key_list[5], (ENC_FF, ENC_D), ENC_FF ** -0.5, 0.078125, ((0, 2),)),
        "enc_fc2_bias": normal_values(key_list[6], (ENC_D,), 0.5, 3.0, (), jnp.float32),
        "handoff_weight": normal_values(key_list[7], (ENC_D, DD), ENC_D ** -0.5, 0.15625),
        "mask_token": normal_values(key_list[8], (DD,), 1.0, 4.0, (), jnp.float32),
        "dec_norm_gain": jnp.clip(1.0 + 0.18 * jax.random.normal(key_list[9], (2, DD), jnp.float32), 0.1, 1.9),
        "qkv_weight": draw_qkv_weight(jax.random.fold_in(key_list[18], 71), 0),
        "qkv_bias": normal_values(key_list[11], (3 * DD,), 0.5, 3.0, (), jnp.float32),
        "out_weight": normal_values(key_list[12], (DD, DD), DD ** -0.5, 0.25),
        "out_bias": normal_values(key_list[13], (DD,), 0.5, 3.0, (), jnp.float32),
        "dec_fc1": normal_values(key_list[14], (DD, DEC_FF), DD ** -0.5, 0.25),
        "dec_fc1_bias": normal_values(key_list[15], (DEC_FF,), 0.5, 3.0, (), jnp.float32),
        "dec_fc2": normal_values(key_list[16], (DEC_FF, DD), DEC_FF ** -0.5, 0.125),
        "dec_fc2_bias": normal_values(key_list[17], (DD,), 0.5, 3.0, (), jnp.float32),
    }


EPS = 1e-06

def layer_norm(values, gain):
    mean = lax.optimization_barrier(jnp.mean(values, axis=-1, keepdims=True))
    centered = values - mean
    spread = lax.optimization_barrier(jnp.mean(centered * centered, axis=-1, keepdims=True))
    return centered * lax.rsqrt(spread + EPS) * gain

def sinusoid(positions, width):
    column = jnp.arange(width)
    exponent = (2 * (column // 2)).astype(jnp.float32) / width
    angle = positions.astype(jnp.float32)[:, None] / jnp.power(jnp.float32(10000.0), exponent)[None, :]
    return jnp.where(column % 2 == 0, jnp.sin(angle), jnp.cos(angle))

def rounded(values):
    return lax.optimization_barrier(values.astype(jnp.bfloat16))

def reference(enc_rows, visible_pos, enc_norm_gain, enc_fc1, enc_fc1_bias, enc_fc2, enc_fc2_bias, handoff_weight, mask_token, dec_norm_gain, qkv_weight, qkv_bias, out_weight, out_bias, dec_fc1, dec_fc1_bias, dec_fc2, dec_fc2_bias):
    resid = enc_rows.astype(jnp.float32)
    normed = layer_norm(resid, enc_norm_gain[0]).astype(jnp.bfloat16)
    hidden = jax.nn.gelu(jnp.dot(normed, enc_fc1, preferred_element_type=jnp.float32) + enc_fc1_bias, approximate=False).astype(jnp.bfloat16)
    encoded = resid + jnp.dot(hidden, enc_fc2, preferred_element_type=jnp.float32) + enc_fc2_bias
    final = layer_norm(encoded, enc_norm_gain[1]).astype(jnp.bfloat16)
    projected = rounded(jnp.dot(final, handoff_weight, preferred_element_type=jnp.float32))
    total_tokens = CLIPS * CLIP_LEN
    placed = jnp.zeros((total_tokens, DD), jnp.float32).at[visible_pos].set(projected.astype(jnp.float32))
    seen = jnp.zeros((total_tokens,), jnp.float32).at[visible_pos].set(1.0)
    stream = placed + (1.0 - seen)[:, None] * mask_token[None, :]
    stream = stream.reshape(CLIPS, CLIP_LEN, DD) + sinusoid(jnp.arange(CLIP_LEN), DD)[None]
    head_d = DD // HEADS
    scale = head_d ** (-0.5)

    def one_clip(clip_stream):
        normed1 = layer_norm(clip_stream, dec_norm_gain[0]).astype(jnp.bfloat16)
        qkv = rounded(jnp.dot(normed1, qkv_weight, preferred_element_type=jnp.float32) + qkv_bias).astype(jnp.float32)
        query = qkv[:, :DD].reshape(CLIP_LEN, HEADS, head_d)
        keys = qkv[:, DD:2 * DD].reshape(CLIP_LEN, HEADS, head_d)
        values = qkv[:, 2 * DD:].reshape(CLIP_LEN, HEADS, head_d)
        scores = jnp.einsum('qhd,khd->hqk', query, keys) * scale
        peak = lax.optimization_barrier(jnp.max(scores, axis=-1, keepdims=True))
        expo = jnp.exp(scores - peak)
        total = lax.optimization_barrier(jnp.sum(expo, axis=-1))
        weights = rounded(expo).astype(jnp.float32)
        mixed = jnp.einsum('hqk,khd->qhd', weights, values) / jnp.transpose(total)[:, :, None]
        attended = mixed.reshape(CLIP_LEN, DD).astype(jnp.bfloat16)
        stream2 = clip_stream + jnp.dot(attended, out_weight, preferred_element_type=jnp.float32) + out_bias
        normed2 = layer_norm(stream2, dec_norm_gain[1]).astype(jnp.bfloat16)
        inner = jax.nn.gelu(jnp.dot(normed2, dec_fc1, preferred_element_type=jnp.float32) + dec_fc1_bias, approximate=False).astype(jnp.bfloat16)
        return (stream2 + jnp.dot(inner, dec_fc2, preferred_element_type=jnp.float32) + dec_fc2_bias).astype(jnp.bfloat16)
    return lax.map(one_clip, stream)
```

```python
import math

import jax
import jax.numpy as jnp
import numpy as np
from jax import lax
from jax.experimental import pallas as pl
from jax.experimental.pallas import tpu as pltpu
from jax.sharding import PartitionSpec as P

HEADS = 8
CLIP_LEN = 2048
SPAN = 1024
WIDTH = 512
HEAD_D = 64
GROUP = 16
LABEL_ROW = 12
EPS = 1e-06
F32 = jnp.float32
BF16 = jnp.bfloat16
MIB = 1 << 20
SAFE = 60.0
SAFE_VALUE = 2.0**40
ERF_COEFS = (
    0.7978726684108748,
    0.03636555646455726,
    -5.779498390881602e-05,
    -4.7281422358059907e-05,
    2.799849175997251e-06,
    -5.6647100069136295e-08,
)
ERF_TOP = 5.5 * 5.5


def norm(values, gain):
    mean = jnp.mean(values, axis=-1, keepdims=True)
    centered = values - mean
    spread = jnp.mean(centered * centered, axis=-1, keepdims=True)
    return centered * lax.rsqrt(spread + EPS) * gain


def gelu(x):
    square = jnp.minimum(x * x, ERF_TOP)
    poly = jnp.full_like(x, ERF_COEFS[-1])
    for coef in ERF_COEFS[-2::-1]:
        poly = poly * square + coef
    half = 0.5 * x
    return half + half * jnp.tanh(x * poly)


def dot(a, b):
    return jnp.dot(a, b, preferred_element_type=F32)


def iota(shape, dim):
    return lax.broadcasted_iota(jnp.int32, shape, dim)


def sinusoid_parts():
    column = np.arange(WIDTH)
    rate = 10000.0 ** (-(2 * (column // 2)) / WIDTH)
    phase = np.where(column % 2 == 0, 0.0, np.pi / 2)
    coarse = 32.0 * np.arange(CLIP_LEN // 32)[:, None] * rate[None, :] + phase[None, :]
    fine = np.arange(32)[:, None] * rate[None, :]
    return tuple(
        np.asarray(part, np.float32)
        for part in (np.sin(coarse), np.cos(coarse), np.sin(fine), np.cos(fine))
    )


ENC_TILE = 512


def enc_kernel(rows_ref, gain_ref, w1_ref, b1_ref, w2_ref, out_ref, normed, total):
    step = pl.program_id(0)

    @pl.when(step == 0)
    def _():
        normed[...] = norm(rows_ref[...].astype(F32), gain_ref[...]).astype(BF16)
        total[...] = jnp.zeros_like(total)

    hidden = gelu(dot(normed[...], w1_ref[...]) + b1_ref[...]).astype(BF16)
    total[...] += dot(hidden, w2_ref[...])

    @pl.when(step == pl.num_programs(0) - 1)
    def _():
        out_ref[...] = total[...].astype(BF16)


def encoder_mlp(rows, gain, w1, b1, w2):
    count, width = rows.shape
    units = w1.shape[1]
    return pl.pallas_call(
        enc_kernel,
        grid=(units // ENC_TILE,),
        in_specs=[
            pl.BlockSpec((count, width), lambda i: (0, 0)),
            pl.BlockSpec((1, width), lambda i: (0, 0)),
            pl.BlockSpec((width, ENC_TILE), lambda i: (0, i)),
            pl.BlockSpec((1, ENC_TILE), lambda i: (0, i)),
            pl.BlockSpec((ENC_TILE, width), lambda i: (i, 0)),
        ],
        out_specs=pl.BlockSpec((count, width), lambda i: (0, 0)),
        out_shape=jax.ShapeDtypeStruct((count, width), BF16),
        scratch_shapes=[pltpu.VMEM((count, width), BF16), pltpu.VMEM((count, width), F32)],
        compiler_params=pltpu.CompilerParams(vmem_limit_bytes=32 * MIB),
        cost_estimate=pl.CostEstimate(
            flops=4 * count * width * units,
            bytes_accessed=4 * width * units + 4 * count * width,
            transcendentals=count * units,
        ),
        name="encoder_mlp",
    )(rows, gain, w1, b1, w2)


def handoff_kernel(seq_ref, pos_ref, own_ref, peer_ref, own_a, own_b, peer_a, peer_b, bias_ref,
                   gain_ref, weight_ref, out_ref):
    tokens = pos_ref.shape[1]

    def project(rows, part_a, part_b):
        encoded = (
            rows[...].astype(F32)
            + (part_a[...].astype(F32) + part_b[...].astype(F32))
            + bias_ref[...]
        )
        final = norm(encoded, gain_ref[...]).astype(BF16)
        return dot(final, weight_ref[...]).astype(BF16)

    projected = jnp.concatenate(
        [project(own_ref, own_a, own_b), project(peer_ref, peer_a, peer_b)], axis=0
    )
    pos = pos_ref[...]
    chosen = ((pos >> 10) & 1) == seq_ref[0]
    clip_row = jnp.where(chosen, pos >> 11, -1).astype(F32)
    label_row = ((pos & (SPAN - 1)) + 1).astype(F32)
    down, across = iota((tokens, tokens), 0), iota((tokens, tokens), 1)
    same = down == across
    clip_col = jnp.sum(jnp.where(same, clip_row, 0.0), axis=1, keepdims=True)
    label_col = jnp.sum(jnp.where(same, label_row, 0.0), axis=1, keepdims=True)
    alike = clip_col == clip_row
    rank_col = jnp.sum(jnp.where(alike & (across < down), 1.0, 0.0), axis=1, keepdims=True)
    rank_row = jnp.sum(jnp.where(alike & (down < across), 1.0, 0.0), axis=0, keepdims=True)
    clips = out_ref.shape[0] // GROUP
    slot_row = jnp.where(clip_row >= 0, clip_row * GROUP + rank_row, -1.0).astype(jnp.int32)
    pick = (iota((clips * GROUP, tokens), 0) == slot_row).astype(F32).astype(BF16)
    packed = dot(pick, projected).astype(BF16).reshape(clips, GROUP, WIDTH)
    to_clip = (iota((clips, tokens), 0) == clip_row.astype(jnp.int32)).astype(F32).astype(BF16)
    upper = jnp.floor(label_col * (1.0 / 32.0))
    lower = label_col - 32.0 * upper
    lane = iota((tokens, 128), 1).astype(F32)
    codes = jnp.where(lane == rank_col, upper, 0.0) + jnp.where(lane == rank_col + 16.0, lower, 0.0)
    labels = dot(to_clip, codes.astype(BF16))
    first = jnp.where(
        iota((clips, GROUP, 128), 1) == LABEL_ROW,
        labels.reshape(clips, 1, 128),
        packed[:, :, :128].astype(F32),
    ).astype(BF16)
    out_ref[:, :128] = first.reshape(clips * GROUP, 128)
    out_ref[:, 128:] = packed[:, :, 128:].reshape(clips * GROUP, WIDTH - 128)


def handoff(seq, pos, own, peer, own_a, own_b, peer_a, peer_b, bias, gain, weight, clips):
    whole = pl.BlockSpec(memory_space=pltpu.VMEM)
    return pl.pallas_call(
        handoff_kernel,
        in_specs=[pl.BlockSpec(memory_space=pltpu.SMEM)] + [whole] * 10,
        out_specs=whole,
        out_shape=jax.ShapeDtypeStruct((clips * GROUP, WIDTH), BF16),
        compiler_params=pltpu.CompilerParams(vmem_limit_bytes=40 * MIB),
        cost_estimate=pl.CostEstimate(
            flops=2 * 512 * (1408 * 512 + 1024 * 512), bytes_accessed=7 * MIB, transcendentals=0
        ),
        name="handoff",
    )(seq, pos, own, peer, own_a, own_b, peer_a, peer_b, bias, gain, weight)


def slot_labels(got_ref):
    slots = got_ref.shape[0]
    clips = slots // GROUP
    head = got_ref[:, :128].astype(F32).reshape(clips, GROUP, 128)
    codes = jnp.sum(jnp.where(iota(head.shape, 1) == LABEL_ROW, head, 0.0), axis=1)
    lane, place = iota((128, slots), 0), iota((128, slots), 1) % GROUP
    spread = jnp.where(lane == place, 32.0, 0.0) + jnp.where(lane == place + 16, 1.0, 0.0)
    by_clip = dot(codes.astype(BF16), spread.astype(BF16))
    mine = iota((clips, slots), 0) == iota((clips, slots), 1) // GROUP
    return jnp.sum(jnp.where(mine, by_clip, 0.0), axis=0, keepdims=True)


def stream_tile(half, first, count, got_ref, label_row, mask, parts):
    slots = got_ref.shape[0]
    want = (iota((count, slots), 0) + (first + 1)).astype(F32)
    place = (want == label_row).astype(F32)
    seen = jnp.sum(place, axis=1, keepdims=True)
    placed = dot(place.astype(BF16), got_ref[...])
    sin_a, cos_a, sin_b, cos_b = parts
    blocks = count // 32
    start = pl.multiple_of(half * (SPAN // 32) + first // 32, 8)
    coarse_sin = sin_a[pl.ds(start, blocks), :].reshape(blocks, 1, WIDTH)
    coarse_cos = cos_a[pl.ds(start, blocks), :].reshape(blocks, 1, WIDTH)
    table = coarse_sin * cos_b[...][None] + coarse_cos * sin_b[...][None]
    return placed + (1.0 - seen) * mask + table.reshape(count, WIDTH)


QKV_TILE = 256


def qkv_kernel(seq_ref, got_ref, sin_a, cos_a, sin_b, cos_b, mask_ref, gain_ref, weight_ref,
               bias_ref, stream_ref, qkv_ref, labels):
    step = pl.program_id(0)

    @pl.when(step == 0)
    def _():
        labels[...] = jnp.broadcast_to(slot_labels(got_ref), labels.shape)

    stream = stream_tile(
        seq_ref[0], step * QKV_TILE, QKV_TILE, got_ref, labels[0:1, :], mask_ref[...],
        (sin_a, cos_a, sin_b, cos_b),
    )
    stream_ref[...] = stream
    normed = norm(stream, gain_ref[...]).astype(BF16)
    out = dot(normed, weight_ref[...]) + bias_ref[...]
    scale = HEAD_D ** (-0.5) * math.log2(math.e)
    qkv_ref[:, :WIDTH] = (out[:, :WIDTH] * scale).astype(BF16)
    qkv_ref[:, WIDTH:] = out[:, WIDTH:].astype(BF16)


def fixed(shape):
    return pl.BlockSpec(shape, lambda i: (0,) * len(shape))


def own_qkv(seq, got, parts, mask, gain, weight, bias):
    return pl.pallas_call(
        qkv_kernel,
        grid=(SPAN // QKV_TILE,),
        in_specs=[pl.BlockSpec(memory_space=pltpu.SMEM), fixed(got.shape)]
        + [fixed(part.shape) for part in parts]
        + [fixed(mask.shape), fixed(gain.shape), fixed(weight.shape), fixed(bias.shape)],
        out_specs=[
            pl.BlockSpec((QKV_TILE, WIDTH), lambda i: (i, 0)),
            pl.BlockSpec((QKV_TILE, 3 * WIDTH), lambda i: (i, 0)),
        ],
        out_shape=[
            jax.ShapeDtypeStruct((SPAN, WIDTH), F32),
            jax.ShapeDtypeStruct((SPAN, 3 * WIDTH), BF16),
        ],
        scratch_shapes=[pltpu.VMEM((8, got.shape[0]), F32)],
        compiler_params=pltpu.CompilerParams(vmem_limit_bytes=32 * MIB),
        cost_estimate=pl.CostEstimate(
            flops=2 * SPAN * WIDTH * (3 * WIDTH + SPAN), bytes_accessed=9 * MIB, transcendentals=0
        ),
        name="own_qkv",
    )(seq, got, *parts, mask, gain, weight, bias)


Q_TILE = 256
KEY_TILE = 512


def decoder_kernel(seq_ref, qkv_ref, stream_ref, got_ref, sin_a, cos_a, sin_b, cos_b, mask_ref,
                   gain_ref, kv_weight_ref, kv_bias_ref, out_weight_ref, out_bias_ref, gain2_ref,
                   fc1_ref, fc1_bias_ref, fc2_ref, fc2_bias_ref, out_ref, keys, values, attended,
                   safe):
    step = pl.program_id(0)
    low = iota((1, 128), 1) < HEAD_D

    @pl.when(step == 0)
    def _():
        label_row = slot_labels(got_ref)
        other = 1 - seq_ref[0]
        for first in range(0, SPAN, QKV_TILE):
            stream = stream_tile(
                other, first, QKV_TILE, got_ref, label_row, mask_ref[...],
                (sin_a, cos_a, sin_b, cos_b),
            )
            normed = norm(stream, gain_ref[...]).astype(BF16)
            out = (dot(normed, kv_weight_ref[...]) + kv_bias_ref[...]).astype(BF16)
            rows = pl.ds(SPAN + first, QKV_TILE)
            keys[rows, :] = out[:, :WIDTH]
            values[rows, : WIDTH] = out[:, WIDTH:]
        keys[:SPAN, :] = qkv_ref[:, WIDTH : 2 * WIDTH]
        values[:SPAN, :WIDTH] = qkv_ref[:, 2 * WIDTH :]
        head_of = (iota((WIDTH, 128), 0) // HEAD_D == iota((WIDTH, 128), 1)).astype(F32).astype(BF16)
        query = qkv_ref[:, :WIDTH].astype(F32)
        key = keys[...].astype(F32)
        q_top = jnp.max(dot((query * query).astype(BF16), head_of), axis=0, keepdims=True)
        k_top = jnp.max(dot((key * key).astype(BF16), head_of), axis=0, keepdims=True)
        score_top = jnp.max(q_top * k_top)
        value_top = jnp.max(jnp.abs(values[:, :WIDTH].astype(F32)))
        safe[0] = ((score_top <= SAFE * SAFE) & (value_top <= SAFE_VALUE)).astype(jnp.int32)

    rows = pl.ds(pl.multiple_of(step * Q_TILE, Q_TILE), Q_TILE)

    def attend(pair, peaked):
        lanes = pl.ds(pair * 128, 128) if isinstance(pair, int) else pl.ds(
            pl.multiple_of(pair * 128, 128), 128
        )
        query = qkv_ref[rows, lanes]
        mixed = []
        for half in range(2):
            own = low if half == 0 else jnp.logical_not(low)
            one_lane = (iota((1, 128), 1) == (HEAD_D if half == 0 else 0)).astype(F32)
            one = jnp.broadcast_to(one_lane, (KEY_TILE, 128)).astype(BF16)
            masked = jnp.where(own, query, jnp.zeros_like(query))

            def score(at):
                return lax.dot_general(
                    masked, keys[at : at + KEY_TILE, lanes], (((1,), (1,)), ((), ())),
                    preferred_element_type=F32,
                )

            starts = range(0, CLIP_LEN, KEY_TILE)
            peak = None
            if peaked:
                for at in starts:
                    top = jnp.max(score(at), axis=-1, keepdims=True)
                    peak = top if peak is None else jnp.maximum(peak, top)
            total = None
            for at in starts:
                scores = score(at)
                if peaked:
                    scores = scores - peak
                weights = jnp.exp2(scores).astype(BF16)
                value = jnp.where(own, values[at : at + KEY_TILE, lanes], one)
                part = dot(weights, value)
                total = part if total is None else total + part
            column = HEAD_D if half == 0 else 0
            mixed.append(total / total[:, column : column + 1])
        attended[:, lanes] = jnp.where(low, mixed[0], mixed[1]).astype(BF16)

    @pl.when(safe[0] == 1)
    def _():
        for pair in range(HEADS // 2):
            attend(pair, False)

    @pl.when(safe[0] != 1)
    def _():
        def one_pair(pair, carry):
            attend(pair, True)
            return carry

        lax.fori_loop(0, HEADS // 2, one_pair, 0)

    stream2 = stream_ref[...] + dot(attended[...], out_weight_ref[...]) + out_bias_ref[...]
    normed2 = norm(stream2, gain2_ref[...]).astype(BF16)
    inner = gelu(dot(normed2, fc1_ref[...]) + fc1_bias_ref[...]).astype(BF16)
    out_ref[...] = (stream2 + dot(inner, fc2_ref[...]) + fc2_bias_ref[...]).astype(BF16)


def decoder(seq, qkv, stream, got, parts, mask, gain, kv_weight, kv_bias, out_weight, out_bias,
            gain2, fc1, fc1_bias, fc2, fc2_bias):
    tail = (mask, gain, kv_weight, kv_bias, out_weight, out_bias, gain2, fc1, fc1_bias, fc2, fc2_bias)
    return pl.pallas_call(
        decoder_kernel,
        grid=(SPAN // Q_TILE,),
        in_specs=[
            pl.BlockSpec(memory_space=pltpu.SMEM),
            fixed(qkv.shape),
            pl.BlockSpec((Q_TILE, WIDTH), lambda i: (i, 0)),
            fixed(got.shape),
        ]
        + [fixed(part.shape) for part in parts]
        + [fixed(item.shape) for item in tail],
        out_specs=pl.BlockSpec((Q_TILE, WIDTH), lambda i: (i, 0)),
        out_shape=jax.ShapeDtypeStruct((SPAN, WIDTH), BF16),
        scratch_shapes=[
            pltpu.VMEM((CLIP_LEN, WIDTH), BF16),
            pltpu.VMEM((CLIP_LEN, WIDTH), BF16),
            pltpu.VMEM((Q_TILE, WIDTH), BF16),
            pltpu.SMEM((1,), jnp.int32),
        ],
        compiler_params=pltpu.CompilerParams(vmem_limit_bytes=56 * MIB),
        cost_estimate=pl.CostEstimate(
            flops=4 * SPAN * CLIP_LEN * WIDTH + 2 * SPAN * WIDTH * (WIDTH + 4096 + 2048),
            bytes_accessed=16 * MIB,
            transcendentals=HEADS * SPAN * CLIP_LEN,
        ),
        name="decoder",
    )(seq, qkv, stream, got, *parts, *tail)


def body(
    enc_rows,
    visible_pos,
    enc_norm_gain,
    enc_fc1,
    enc_fc1_bias,
    enc_fc2,
    enc_fc2_bias,
    handoff_weight,
    mask_token,
    dec_norm_gain,
    qkv_weight,
    qkv_bias,
    out_weight,
    out_bias,
    dec_fc1,
    dec_fc1_bias,
    dec_fc2,
    dec_fc2_bias,
):
    def swap(values):
        return lax.ppermute(values, "seq", [(0, 1), (1, 0)])

    def row(values):
        return values.reshape(1, -1)

    clips = lax.axis_size("rows")
    seq = lax.axis_index("seq").astype(jnp.int32).reshape(1)
    parts = tuple(jnp.asarray(part) for part in sinusoid_parts())
    gain = row(enc_norm_gain[0])
    bias1 = row(enc_fc1_bias)
    peer_rows = swap(enc_rows)
    pos = jnp.concatenate([visible_pos, swap(visible_pos)]).reshape(1, -1)
    own_part = encoder_mlp(enc_rows, gain, enc_fc1, bias1, enc_fc2)
    peer_rows, own_part = lax.optimization_barrier((peer_rows, own_part))
    peer_part = encoder_mlp(peer_rows, gain, enc_fc1, bias1, enc_fc2)
    payload = handoff(
        seq, pos, enc_rows, peer_rows, own_part, swap(peer_part), peer_part, swap(own_part),
        row(enc_fc2_bias), row(enc_norm_gain[1]), handoff_weight, clips,
    )
    got = lax.all_to_all(
        payload.reshape(clips, GROUP, WIDTH), "rows", split_axis=0, concat_axis=0, tiled=True
    ).reshape(clips * GROUP, WIDTH)
    mask = row(mask_token)
    gain1 = row(dec_norm_gain[0])
    peer_got = swap(got)
    stream, qkv = own_qkv(seq, got, parts, mask, gain1, qkv_weight, row(qkv_bias))
    decoded = decoder(
        seq, qkv, stream, peer_got, parts, mask, gain1, qkv_weight[:, WIDTH:],
        row(qkv_bias[WIDTH:]), out_weight, row(out_bias), row(dec_norm_gain[1]), dec_fc1,
        row(dec_fc1_bias), dec_fc2, row(dec_fc2_bias),
    )
    return decoded.reshape(1, SPAN, WIDTH)


def solution(mesh):
    return jax.shard_map(
        body,
        mesh=mesh,
        in_specs=(
            P(("rows", "seq"), None),
            P(("rows", "seq")),
            P(),
            P(None, "seq"),
            P("seq"),
            P("seq", None),
            P(),
            P(),
            P(),
            P(),
            P(),
            P(),
            P(),
            P(),
            P(),
            P(),
            P(),
            P(),
        ),
        out_specs=P("rows", "seq", None),
        check_vma=False,
    )
```

```python
import math

import jax
import jax.numpy as jnp
import numpy as np
from jax import lax
from jax.experimental import pallas as pl
from jax.experimental.pallas import tpu as pltpu
from jax.sharding import PartitionSpec as P

HEADS = 8
CLIP_LEN = 2048
SPAN = 1024
WIDTH = 512
HEAD_D = 64
GROUP = 16
LABEL_ROW = 12
EPS = 1e-06
F32 = jnp.float32
BF16 = jnp.bfloat16
MIB = 1 << 20
WHOLE = pl.BlockSpec(memory_space=pltpu.VMEM)
SAFE = 60.0
SAFE_VALUE = 2.0**40

def norm(values, gain):
    mean = jnp.mean(values, axis=-1, keepdims=True)
    centered = values - mean
    spread = jnp.mean(centered * centered, axis=-1, keepdims=True)
    return centered * lax.rsqrt(spread + EPS) * gain


def gelu(x):
    half = 0.5 * x
    return half + half * lax.erf(x * (0.5**0.5))


def dot(a, b):
    return jnp.dot(a, b, preferred_element_type=F32)


def iota(shape, dim):
    return lax.broadcasted_iota(jnp.int32, shape, dim)


def sinusoid_parts():
    column = np.arange(WIDTH)
    rate = 10000.0 ** (-(2 * (column // 2)) / WIDTH)
    phase = np.where(column % 2 == 0, 0.0, np.pi / 2)
    coarse = 32.0 * np.arange(CLIP_LEN // 32)[:, None] * rate[None, :] + phase[None, :]
    fine = np.arange(32)[:, None] * rate[None, :]
    return tuple(
        np.asarray(part, np.float32)
        for part in (np.sin(coarse), np.cos(coarse), np.sin(fine), np.cos(fine))
    )


ENC_TILE = 512
IN_FLIGHT = 2
IN_SIZES = (1024, 2048)
OUT_SIZES = (1408,)


def tiles_of(sizes):
    starts = [sum(sizes[:i]) for i in range(len(sizes))]
    return [(start, start + size) for start, size in zip(starts, sizes)]


def cut(start, stop):
    return [pl.ds(at, min(ENC_TILE, stop - at)) for at in range(start, stop, ENC_TILE)]


def enc_kernel(rows_ref, gain_ref, w1_ref, b1_ref, w2_ref, out_ref, w1, w2, rows, gain, b1, hidden,
               arrived, arrived1, arrived2):
    small = [
        pltpu.make_async_copy(source, target, arrived.at[i])
        for i, (source, target) in enumerate(((rows_ref, rows), (gain_ref, gain), (b1_ref, b1)))
    ]
    loads = []
    for sizes, source, target, sems in ((IN_SIZES, w1_ref, w1, arrived1), (OUT_SIZES, w2_ref, w2, arrived2)):
        for i, (start, stop) in enumerate(tiles_of(sizes)):
            tile = pl.ds(start, stop - start)
            loads.append(pltpu.make_async_copy(source.at[:, tile], target.at[:, tile], sems.at[i]))
    for load in small + loads[:IN_FLIGHT]:
        load.start()

    def take(i):
        loads[i].wait()
        if i + IN_FLIGHT < len(loads):
            loads[i + IN_FLIGHT].start()

    for load in small:
        load.wait()
    normed = norm(rows[...].astype(F32), gain[0:1, :]).astype(BF16)
    for i, (start, stop) in enumerate(tiles_of(IN_SIZES)):
        take(i)
        for tile in cut(start, stop):
            hidden[:, tile] = gelu(dot(normed, w1[:, tile]) + b1[:, tile]).astype(BF16)
    for i, (start, stop) in enumerate(tiles_of(OUT_SIZES)):
        take(len(IN_SIZES) + i)
        for tile in cut(start, stop):
            out_ref[:, tile] = dot(hidden[...], w2[:, tile]).astype(BF16)


def enc_cost(count, width, units):
    return pl.CostEstimate(
        flops=4 * count * width * units,
        bytes_accessed=4 * width * units + 4 * count * width,
        transcendentals=count * units,
    )


def first_encoder_mlp(rows, gain, w1, b1, w2):
    count, width = rows.shape
    units = w1.shape[1]
    far = pl.BlockSpec(memory_space=pl.ANY)
    return pl.pallas_call(
        enc_kernel,
        in_specs=[far] * 5,
        out_specs=[WHOLE] * 3,
        out_shape=[
            jax.ShapeDtypeStruct((count, width), BF16),
            jax.ShapeDtypeStruct(w1.shape, BF16),
            jax.ShapeDtypeStruct(w2.shape, BF16),
        ],
        scratch_shapes=[
            pltpu.VMEM((count, width), BF16),
            pltpu.VMEM(gain.shape, F32),
            pltpu.VMEM(b1.shape, F32),
            pltpu.VMEM((count, units), BF16),
            pltpu.SemaphoreType.DMA((3,)),
            pltpu.SemaphoreType.DMA((len(IN_SIZES),)),
            pltpu.SemaphoreType.DMA((len(OUT_SIZES),)),
        ],
        compiler_params=pltpu.CompilerParams(vmem_limit_bytes=ENC_VMEM * MIB),
        cost_estimate=enc_cost(count, width, units),
        name="first_encoder_mlp",
    )(rows, gain, w1, b1, w2)


def second_enc_kernel(rows_ref, gain_ref, w1, b1, w2, out_ref, hidden):
    units, width = w2.shape
    normed = norm(rows_ref[...].astype(F32), gain_ref[0:1, :]).astype(BF16)
    for tile in cut(0, units):
        hidden[:, tile] = gelu(dot(normed, w1[:, tile]) + b1[:, tile]).astype(BF16)
    for tile in cut(0, width):
        out_ref[:, tile] = dot(hidden[...], w2[:, tile]).astype(BF16)


def second_encoder_mlp(rows, gain, w1, b1, w2):
    count, width = rows.shape
    units = w1.shape[1]
    return pl.pallas_call(
        second_enc_kernel,
        in_specs=[WHOLE] * 5,
        out_specs=WHOLE,
        out_shape=jax.ShapeDtypeStruct((count, width), BF16),
        scratch_shapes=[pltpu.VMEM((count, units), BF16)],
        compiler_params=pltpu.CompilerParams(vmem_limit_bytes=ENC_VMEM * MIB),
        cost_estimate=enc_cost(count, width, units),
        name="second_encoder_mlp",
    )(rows, gain, w1, b1, w2)
ENC_VMEM = 16


def project(rows, part_a, part_b, bias_ref, gain_ref, weight_ref):
    encoded = (
        rows[...].astype(F32) + (part_a[...].astype(F32) + part_b[...].astype(F32)) + bias_ref[...]
    )
    final = norm(encoded, gain_ref[1:2, :]).astype(BF16)
    return dot(final, weight_ref[...]).astype(BF16)


def project_kernel(rows, part_a, part_b, bias_ref, gain_ref, weight_ref, out_ref):
    out_ref[...] = project(rows, part_a, part_b, bias_ref, gain_ref, weight_ref)


def projection(rows, part_a, part_b, bias, gain, weight):
    return pl.pallas_call(
        project_kernel,
        in_specs=[WHOLE] * 6,
        out_specs=WHOLE,
        out_shape=jax.ShapeDtypeStruct((rows.shape[0], WIDTH), BF16),
        compiler_params=pltpu.CompilerParams(vmem_limit_bytes=16 * MIB),
        cost_estimate=pl.CostEstimate(
            flops=2 * rows.size * WIDTH, bytes_accessed=4 * MIB, transcendentals=0
        ),
        name="projection",
    )(rows, part_a, part_b, bias, gain, weight)


def handoff_kernel(seq_ref, pos_ref, own_ref, own_a, own_b, bias_ref, gain_ref, weight_ref,
                   peer_ref, out_ref):
    tokens = pos_ref.shape[1]
    own = project(own_ref, own_a, own_b, bias_ref, gain_ref, weight_ref)
    projected = jnp.concatenate([own, peer_ref[...]], axis=0)
    pos = pos_ref[...]
    chosen = ((pos >> 10) & 1) == seq_ref[0]
    clip_row = jnp.where(chosen, pos >> 11, -1).astype(F32)
    label_row = ((pos & (SPAN - 1)) + 1).astype(F32)
    down, across = iota((tokens, tokens), 0), iota((tokens, tokens), 1)
    same = down == across
    clip_col = jnp.sum(jnp.where(same, clip_row, 0.0), axis=1, keepdims=True)
    label_col = jnp.sum(jnp.where(same, label_row, 0.0), axis=1, keepdims=True)
    alike = clip_col == clip_row
    rank_col = jnp.sum(jnp.where(alike & (across < down), 1.0, 0.0), axis=1, keepdims=True)
    rank_row = jnp.sum(jnp.where(alike & (down < across), 1.0, 0.0), axis=0, keepdims=True)
    clips = out_ref.shape[0] // GROUP
    slot_row = jnp.where(clip_row >= 0, clip_row * GROUP + rank_row, -1.0).astype(jnp.int32)
    pick = (iota((clips * GROUP, tokens), 0) == slot_row).astype(F32).astype(BF16)
    packed = dot(pick, projected).astype(BF16).reshape(clips, GROUP, WIDTH)
    to_clip = (iota((clips, tokens), 0) == clip_row.astype(jnp.int32)).astype(F32).astype(BF16)
    upper = jnp.floor(label_col * (1.0 / 32.0))
    lower = label_col - 32.0 * upper
    lane = iota((tokens, 128), 1).astype(F32)
    codes = jnp.where(lane == rank_col, upper, 0.0) + jnp.where(lane == rank_col + 16.0, lower, 0.0)
    labels = dot(to_clip, codes.astype(BF16))
    first = jnp.where(
        iota((clips, GROUP, 128), 1) == LABEL_ROW,
        labels.reshape(clips, 1, 128),
        packed[:, :, :128].astype(F32),
    ).astype(BF16)
    out_ref[:, :128] = first.reshape(clips * GROUP, 128)
    out_ref[:, 128:] = packed[:, :, 128:].reshape(clips * GROUP, WIDTH - 128)


def handoff(seq, pos, own, own_a, own_b, bias, gain, weight, peer, clips):
    return pl.pallas_call(
        handoff_kernel,
        in_specs=[pl.BlockSpec(memory_space=pltpu.SMEM)] + [WHOLE] * 8,
        out_specs=WHOLE,
        out_shape=jax.ShapeDtypeStruct((clips * GROUP, WIDTH), BF16),
        compiler_params=pltpu.CompilerParams(vmem_limit_bytes=24 * MIB),
        cost_estimate=pl.CostEstimate(
            flops=2 * 512 * (704 * 512 + 1024 * 512), bytes_accessed=7 * MIB, transcendentals=0
        ),
        name="handoff",
    )(seq, pos, own, own_a, own_b, bias, gain, weight, peer)


def slot_labels(got_ref):
    slots = got_ref.shape[0]
    clips = slots // GROUP
    head = got_ref[:, :128].astype(F32).reshape(clips, GROUP, 128)
    codes = jnp.sum(jnp.where(iota(head.shape, 1) == LABEL_ROW, head, 0.0), axis=1)
    lane, place = iota((128, slots), 0), iota((128, slots), 1) % GROUP
    spread = jnp.where(lane == place, 32.0, 0.0) + jnp.where(lane == place + 16, 1.0, 0.0)
    by_clip = dot(codes.astype(BF16), spread.astype(BF16))
    mine = iota((clips, slots), 0) == iota((clips, slots), 1) // GROUP
    return jnp.sum(jnp.where(mine, by_clip, 0.0), axis=0, keepdims=True)


def stream_tile(half, first, count, got_ref, label_row, mask, parts):
    slots = got_ref.shape[0]
    want = (iota((count, slots), 0) + (first + 1)).astype(F32)
    place = (want == label_row).astype(F32)
    seen = jnp.sum(place, axis=1, keepdims=True)
    placed = dot(place.astype(BF16), got_ref[...])
    sin_a, cos_a, sin_b, cos_b = parts
    blocks = count // 32
    start = pl.multiple_of(half * (SPAN // 32) + first // 32, 8)
    coarse_sin = sin_a[pl.ds(start, blocks), :].reshape(blocks, 1, WIDTH)
    coarse_cos = cos_a[pl.ds(start, blocks), :].reshape(blocks, 1, WIDTH)
    table = coarse_sin * cos_b[...][None] + coarse_cos * sin_b[...][None]
    return placed + (1.0 - seen) * mask + table.reshape(count, WIDTH)


QKV_TILE = 512


def qkv_kernel(seq_ref, got_ref, sin_a, cos_a, sin_b, cos_b, mask_ref, gain_ref, weight_ref,
               bias_ref, stream_ref, query_ref, key_ref, value_ref):
    label_row = slot_labels(got_ref)
    scale = HEAD_D ** (-0.5) * math.log2(math.e)
    for first in range(0, SPAN, QKV_TILE):
        rows = pl.ds(first, QKV_TILE)
        stream = stream_tile(
            seq_ref[0], first, QKV_TILE, got_ref, label_row, mask_ref[...],
            (sin_a, cos_a, sin_b, cos_b),
        )
        stream_ref[rows, :] = stream
        normed = norm(stream, gain_ref[0:1, :]).astype(BF16)
        out = dot(normed, weight_ref[...]) + bias_ref[...]
        query_ref[rows, :] = (out[:, :WIDTH] * scale).astype(BF16)
        key_ref[rows, :] = out[:, WIDTH : 2 * WIDTH].astype(BF16)
        value_ref[:, rows] = out[:, 2 * WIDTH :].T.astype(BF16)


def own_qkv(seq, got, parts, mask, gain, weight, bias):
    return pl.pallas_call(
        qkv_kernel,
        in_specs=[pl.BlockSpec(memory_space=pltpu.SMEM)] + [WHOLE] * 9,
        out_specs=[WHOLE] * 4,
        out_shape=[
            jax.ShapeDtypeStruct((SPAN, WIDTH), F32),
            jax.ShapeDtypeStruct((SPAN, WIDTH), BF16),
            jax.ShapeDtypeStruct((SPAN, WIDTH), BF16),
            jax.ShapeDtypeStruct((WIDTH, SPAN), BF16),
        ],
        compiler_params=pltpu.CompilerParams(vmem_limit_bytes=20 * MIB),
        cost_estimate=pl.CostEstimate(
            flops=2 * SPAN * WIDTH * (3 * WIDTH + SPAN), bytes_accessed=9 * MIB, transcendentals=0
        ),
        name="own_qkv",
    )(seq, got, *parts, mask, gain, weight, bias)


ROW_TILE = 512
FF_TILE = 512


def decoder_kernel(seq_ref, query_ref, key_ref, value_ref, stream_ref, got_ref, sin_a, cos_a,
                   sin_b, cos_b, mask_ref, gain_ref, weight_ref, bias_ref, out_weight_ref,
                   out_bias_ref, fc1_ref, fc1_bias_ref, fc2_ref, fc2_bias_ref, out_ref, peer_key,
                   peer_value, attended, hidden):
    label_row = slot_labels(got_ref)
    other = 1 - seq_ref[0]
    for first in range(0, SPAN, QKV_TILE):
        rows = pl.ds(first, QKV_TILE)
        stream = stream_tile(
            other, first, QKV_TILE, got_ref, label_row, mask_ref[...],
            (sin_a, cos_a, sin_b, cos_b),
        )
        normed = norm(stream, gain_ref[0:1, :]).astype(BF16)
        out = dot(normed, weight_ref[:, WIDTH:]) + bias_ref[:, WIDTH:]
        peer_key[rows, :] = out[:, :WIDTH].astype(BF16)
        peer_value[:, rows] = out[:, WIDTH:].T.astype(BF16)

    head_of = (iota((WIDTH, 128), 0) // HEAD_D == iota((WIDTH, 128), 1)).astype(F32).astype(BF16)

    def top(ref):
        return jnp.max(dot(ref[...] * ref[...], head_of), axis=0, keepdims=True)

    def largest(ref):
        return jnp.max(jnp.abs(ref[...].astype(F32)))

    score_top = jnp.max(top(query_ref) * jnp.maximum(top(key_ref), top(peer_key)))
    value_top = jnp.maximum(largest(value_ref), largest(peer_value))
    safe = (score_top <= SAFE * SAFE) & (value_top <= SAFE_VALUE)
    halves = ((key_ref, value_ref), (peer_key, peer_value))

    def attend(pair, peaked):
        lanes = pl.ds(pl.multiple_of(pair * 128, 128), 128)
        query = query_ref[:, lanes]
        mixed = []
        for half in range(2):
            own_lane = (iota((1, 128), 1) < HEAD_D) == (half == 0)
            own_row = (iota((128, 1), 0) < HEAD_D) == (half == 0)
            masked = jnp.where(own_lane, query, jnp.zeros_like(query))

            def score(keys):
                return lax.dot_general(
                    keys[:, lanes], masked, (((1,), (1,)), ((), ())), preferred_element_type=F32
                )

            if peaked:
                peak = jnp.maximum(
                    *(jnp.max(score(keys), axis=0, keepdims=True) for keys, _ in halves)
                )
            total = None
            for keys, values in halves:
                scores = score(keys)
                if peaked:
                    scores = scores - peak
                weights = jnp.exp2(scores).astype(BF16)
                value = values[lanes, :]
                value = jnp.where(own_row, value, jnp.ones_like(value))
                part = dot(value, weights)
                total = part if total is None else total + part
            mixed.append(total)
        first = mixed[0][:HEAD_D] / mixed[0][HEAD_D:]
        second = mixed[1][HEAD_D:] / mixed[1][:HEAD_D]
        attended[:, lanes] = jnp.concatenate([first, second], axis=0).T.astype(BF16)

    def all_heads(peaked):
        def one_pair(pair, carry):
            attend(pair, peaked)
            return carry

        lax.fori_loop(0, HEADS // 2, one_pair, 0)

    @pl.when(safe)
    def _():
        all_heads(False)

    @pl.when(jnp.logical_not(safe))
    def _():
        all_heads(True)

    for first in range(0, SPAN, ROW_TILE):
        rows = pl.ds(first, ROW_TILE)
        stream2 = stream_ref[rows, :] + dot(attended[rows, :], out_weight_ref[...]) + out_bias_ref[...]
        normed2 = norm(stream2, gain_ref[1:2, :]).astype(BF16)
        for at in range(0, hidden.shape[1], FF_TILE):
            units = pl.ds(at, FF_TILE)
            inner = dot(normed2, fc1_ref[:, units]) + fc1_bias_ref[:, units]
            hidden[:, units] = gelu(inner).astype(BF16)
        out_ref[rows, :] = (stream2 + dot(hidden[...], fc2_ref[...]) + fc2_bias_ref[...]).astype(BF16)


def decoder(seq, query, key, value, stream, got, parts, mask, gain, weight, bias, out_weight,
            out_bias, fc1, fc1_bias, fc2, fc2_bias):
    tail = (mask, gain, weight, bias, out_weight, out_bias, fc1, fc1_bias, fc2, fc2_bias)
    return pl.pallas_call(
        decoder_kernel,
        in_specs=[pl.BlockSpec(memory_space=pltpu.SMEM)] + [WHOLE] * (5 + len(parts) + len(tail)),
        out_specs=WHOLE,
        out_shape=jax.ShapeDtypeStruct((SPAN, WIDTH), BF16),
        scratch_shapes=[
            pltpu.VMEM((SPAN, WIDTH), BF16),
            pltpu.VMEM((WIDTH, SPAN), BF16),
            pltpu.VMEM((SPAN, WIDTH), BF16),
            pltpu.VMEM((ROW_TILE, fc1.shape[1]), BF16),
        ],
        compiler_params=pltpu.CompilerParams(vmem_limit_bytes=DEC_VMEM * MIB),
        cost_estimate=pl.CostEstimate(
            flops=4 * SPAN * CLIP_LEN * WIDTH + 2 * SPAN * WIDTH * (WIDTH + 4096 + 2048),
            bytes_accessed=16 * MIB,
            transcendentals=HEADS * SPAN * CLIP_LEN,
        ),
        name="decoder",
    )(seq, query, key, value, stream, got, *parts, *tail)


DEC_VMEM = 32


def body(
    enc_rows,
    visible_pos,
    enc_norm_gain,
    enc_fc1,
    enc_fc1_bias,
    enc_fc2,
    enc_fc2_bias,
    handoff_weight,
    mask_token,
    dec_norm_gain,
    qkv_weight,
    qkv_bias,
    out_weight,
    out_bias,
    dec_fc1,
    dec_fc1_bias,
    dec_fc2,
    dec_fc2_bias,
):
    def swap(values):
        return lax.ppermute(values, "seq", [(0, 1), (1, 0)])

    def row(values):
        return values.reshape(1, -1)

    clips = lax.axis_size("rows")
    seq = lax.axis_index("seq").astype(jnp.int32).reshape(1)
    parts = tuple(jnp.asarray(part) for part in sinusoid_parts())
    bias1, bias2 = row(enc_fc1_bias), row(enc_fc2_bias)
    peer_rows = swap(enc_rows)
    peer_pos = swap(visible_pos)
    own_part, fc1_here, fc2_here = first_encoder_mlp(enc_rows, enc_norm_gain, enc_fc1, bias1, enc_fc2)
    peer_rows, peer_pos, own_part = lax.optimization_barrier((peer_rows, peer_pos, own_part))
    peer_part = second_encoder_mlp(peer_rows, enc_norm_gain, fc1_here, bias1, fc2_here)
    pos = jnp.concatenate([visible_pos, peer_pos]).reshape(1, -1)
    peer = projection(peer_rows, peer_part, swap(own_part), bias2, enc_norm_gain, handoff_weight)
    payload = handoff(
        seq, pos, enc_rows, own_part, swap(peer_part), bias2, enc_norm_gain, handoff_weight, peer, clips
    )
    got = lax.all_to_all(
        payload.reshape(clips, GROUP, WIDTH), "rows", split_axis=0, concat_axis=0, tiled=True
    ).reshape(clips * GROUP, WIDTH)
    mask = row(mask_token)
    qkv_bias = row(qkv_bias)
    peer_got = swap(got)
    stream, query, key, value = own_qkv(
        seq, got, parts, mask, dec_norm_gain, qkv_weight, qkv_bias
    )
    decoded = decoder(
        seq, query, key, value, stream, peer_got, parts, mask, dec_norm_gain, qkv_weight, qkv_bias,
        out_weight, row(out_bias), dec_fc1, row(dec_fc1_bias), dec_fc2, row(dec_fc2_bias),
    )
    return decoded.reshape(1, SPAN, WIDTH)


def solution(mesh):
    return jax.shard_map(
        body,
        mesh=mesh,
        in_specs=(
            P(("rows", "seq"), None),
            P(("rows", "seq")),
            P(),
            P(None, "seq"),
            P("seq"),
            P("seq", None),
            P(),
            P(),
            P(),
            P(),
            P(),
            P(),
            P(),
            P(),
            P(),
            P(),
            P(),
            P(),
        ),
        out_specs=P("rows", "seq", None),
        check_vma=False,
    )
```

```python
import math

import jax
import jax.numpy as jnp
import numpy as np
from jax import lax
from jax.experimental import pallas as pl
from jax.experimental.pallas import tpu as pltpu
from jax.sharding import PartitionSpec as P

HEADS = 8
CLIP_LEN = 2048
SPAN = 1024
WIDTH = 512
HEAD_D = 64
GROUP = 16
LABEL_ROW = 12
EPS = 1e-06
F32 = jnp.float32
BF16 = jnp.bfloat16
MIB = 1 << 20
WHOLE = pl.BlockSpec(memory_space=pltpu.VMEM)
SAFE = 60.0
SAFE_VALUE = 2.0**40

def norm(values, gain):
    mean = jnp.mean(values, axis=-1, keepdims=True)
    centered = values - mean
    spread = jnp.mean(centered * centered, axis=-1, keepdims=True)
    return centered * lax.rsqrt(spread + EPS) * gain


def gelu(x):
    half = 0.5 * x
    return half + half * lax.erf(x * (0.5**0.5))


def dot(a, b):
    return jnp.dot(a, b, preferred_element_type=F32)


def iota(shape, dim):
    return lax.broadcasted_iota(jnp.int32, shape, dim)


def sinusoid_parts():
    column = np.arange(WIDTH)
    rate = 10000.0 ** (-(2 * (column // 2)) / WIDTH)
    phase = np.where(column % 2 == 0, 0.0, np.pi / 2)
    coarse = 32.0 * np.arange(CLIP_LEN // 32)[:, None] * rate[None, :] + phase[None, :]
    fine = np.arange(32)[:, None] * rate[None, :]
    return tuple(
        np.asarray(part, np.float32)
        for part in (np.sin(coarse), np.cos(coarse), np.sin(fine), np.cos(fine))
    )


ENC_TILE = 512
IN_FLIGHT = 2
IN_SIZES = (1024, 2048)
OUT_SIZES = (1408,)


def tiles_of(sizes):
    starts = [sum(sizes[:i]) for i in range(len(sizes))]
    return [(start, start + size) for start, size in zip(starts, sizes)]


def cut(start, stop):
    return [pl.ds(at, min(ENC_TILE, stop - at)) for at in range(start, stop, ENC_TILE)]


def enc_kernel(rows_ref, gain_ref, w1_ref, b1_ref, w2_ref, out_ref, w1, w2, rows, gain, b1, hidden,
               arrived, arrived1, arrived2):
    small = [
        pltpu.make_async_copy(source, target, arrived.at[i])
        for i, (source, target) in enumerate(((rows_ref, rows), (gain_ref, gain), (b1_ref, b1)))
    ]
    loads = []
    for sizes, source, target, sems in ((IN_SIZES, w1_ref, w1, arrived1), (OUT_SIZES, w2_ref, w2, arrived2)):
        for i, (start, stop) in enumerate(tiles_of(sizes)):
            tile = pl.ds(start, stop - start)
            loads.append(pltpu.make_async_copy(source.at[:, tile], target.at[:, tile], sems.at[i]))
    for load in small + loads[:IN_FLIGHT]:
        load.start()

    def take(i):
        loads[i].wait()
        if i + IN_FLIGHT < len(loads):
            loads[i + IN_FLIGHT].start()

    for load in small:
        load.wait()
    normed = norm(rows[...].astype(F32), gain[0:1, :]).astype(BF16)
    for i, (start, stop) in enumerate(tiles_of(IN_SIZES)):
        take(i)
        for tile in cut(start, stop):
            hidden[:, tile] = gelu(dot(normed, w1[:, tile]) + b1[:, tile]).astype(BF16)
    for i, (start, stop) in enumerate(tiles_of(OUT_SIZES)):
        take(len(IN_SIZES) + i)
        for tile in cut(start, stop):
            out_ref[:, tile] = dot(hidden[...], w2[:, tile]).astype(BF16)


def enc_cost(count, width, units):
    return pl.CostEstimate(
        flops=4 * count * width * units,
        bytes_accessed=4 * width * units + 4 * count * width,
        transcendentals=count * units,
    )


def first_encoder_mlp(rows, gain, w1, b1, w2):
    count, width = rows.shape
    units = w1.shape[1]
    far = pl.BlockSpec(memory_space=pl.ANY)
    return pl.pallas_call(
        enc_kernel,
        in_specs=[far] * 5,
        out_specs=[WHOLE] * 3,
        out_shape=[
            jax.ShapeDtypeStruct((count, width), BF16),
            jax.ShapeDtypeStruct(w1.shape, BF16),
            jax.ShapeDtypeStruct(w2.shape, BF16),
        ],
        scratch_shapes=[
            pltpu.VMEM((count, width), BF16),
            pltpu.VMEM(gain.shape, F32),
            pltpu.VMEM(b1.shape, F32),
            pltpu.VMEM((count, units), BF16),
            pltpu.SemaphoreType.DMA((3,)),
            pltpu.SemaphoreType.DMA((len(IN_SIZES),)),
            pltpu.SemaphoreType.DMA((len(OUT_SIZES),)),
        ],
        compiler_params=pltpu.CompilerParams(vmem_limit_bytes=FIRST_VMEM),
        cost_estimate=enc_cost(count, width, units),
        name="first_encoder_mlp",
    )(rows, gain, w1, b1, w2)


def second_enc_kernel(rows_ref, gain_ref, w1, b1, w2, out_ref, hidden):
    units, width = w2.shape
    normed = norm(rows_ref[...].astype(F32), gain_ref[0:1, :]).astype(BF16)
    for tile in cut(0, units):
        hidden[:, tile] = gelu(dot(normed, w1[:, tile]) + b1[:, tile]).astype(BF16)
    for tile in cut(0, width):
        out_ref[:, tile] = dot(hidden[...], w2[:, tile]).astype(BF16)


def second_encoder_mlp(rows, gain, w1, b1, w2):
    count, width = rows.shape
    units = w1.shape[1]
    return pl.pallas_call(
        second_enc_kernel,
        in_specs=[WHOLE] * 5,
        out_specs=WHOLE,
        out_shape=jax.ShapeDtypeStruct((count, width), BF16),
        scratch_shapes=[pltpu.VMEM((count, units), BF16)],
        compiler_params=pltpu.CompilerParams(vmem_limit_bytes=ENC_VMEM * MIB),
        cost_estimate=enc_cost(count, width, units),
        name="second_encoder_mlp",
    )(rows, gain, w1, b1, w2)
ENC_VMEM = 16
FIRST_VMEM = 34 * MIB


def project(rows, part_a, part_b, bias_ref, gain_ref, weight_ref):
    encoded = (
        rows[...].astype(F32) + (part_a[...].astype(F32) + part_b[...].astype(F32)) + bias_ref[...]
    )
    final = norm(encoded, gain_ref[1:2, :]).astype(BF16)
    return dot(final, weight_ref[...]).astype(BF16)


def project_kernel(rows, part_a, part_b, bias_ref, gain_ref, weight_ref, out_ref):
    out_ref[...] = project(rows, part_a, part_b, bias_ref, gain_ref, weight_ref)


def projection(rows, part_a, part_b, bias, gain, weight):
    return pl.pallas_call(
        project_kernel,
        in_specs=[WHOLE] * 6,
        out_specs=WHOLE,
        out_shape=jax.ShapeDtypeStruct((rows.shape[0], WIDTH), BF16),
        compiler_params=pltpu.CompilerParams(vmem_limit_bytes=16 * MIB),
        cost_estimate=pl.CostEstimate(
            flops=2 * rows.size * WIDTH, bytes_accessed=4 * MIB, transcendentals=0
        ),
        name="projection",
    )(rows, part_a, part_b, bias, gain, weight)


def handoff_kernel(seq_ref, pos_ref, own_ref, own_a, own_b, bias_ref, gain_ref, weight_ref,
                   peer_ref, out_ref):
    tokens = pos_ref.shape[1]
    own = project(own_ref, own_a, own_b, bias_ref, gain_ref, weight_ref)
    projected = jnp.concatenate([own, peer_ref[...]], axis=0)
    pos = pos_ref[...]
    chosen = ((pos >> 10) & 1) == seq_ref[0]
    clip_row = jnp.where(chosen, pos >> 11, -1).astype(F32)
    label_row = ((pos & (SPAN - 1)) + 1).astype(F32)
    down, across = iota((tokens, tokens), 0), iota((tokens, tokens), 1)
    same = down == across
    clip_col = jnp.sum(jnp.where(same, clip_row, 0.0), axis=1, keepdims=True)
    label_col = jnp.sum(jnp.where(same, label_row, 0.0), axis=1, keepdims=True)
    alike = clip_col == clip_row
    rank_col = jnp.sum(jnp.where(alike & (across < down), 1.0, 0.0), axis=1, keepdims=True)
    rank_row = jnp.sum(jnp.where(alike & (down < across), 1.0, 0.0), axis=0, keepdims=True)
    clips = out_ref.shape[0] // GROUP
    slot_row = jnp.where(clip_row >= 0, clip_row * GROUP + rank_row, -1.0).astype(jnp.int32)
    pick = (iota((clips * GROUP, tokens), 0) == slot_row).astype(F32).astype(BF16)
    packed = dot(pick, projected).astype(BF16).reshape(clips, GROUP, WIDTH)
    to_clip = (iota((clips, tokens), 0) == clip_row.astype(jnp.int32)).astype(F32).astype(BF16)
    upper = jnp.floor(label_col * (1.0 / 32.0))
    lower = label_col - 32.0 * upper
    lane = iota((tokens, 128), 1).astype(F32)
    codes = jnp.where(lane == rank_col, upper, 0.0) + jnp.where(lane == rank_col + 16.0, lower, 0.0)
    labels = dot(to_clip, codes.astype(BF16))
    first = jnp.where(
        iota((clips, GROUP, 128), 1) == LABEL_ROW,
        labels.reshape(clips, 1, 128),
        packed[:, :, :128].astype(F32),
    ).astype(BF16)
    out_ref[:, :128] = first.reshape(clips * GROUP, 128)
    out_ref[:, 128:] = packed[:, :, 128:].reshape(clips * GROUP, WIDTH - 128)


def handoff(seq, pos, own, own_a, own_b, bias, gain, weight, peer, clips):
    return pl.pallas_call(
        handoff_kernel,
        in_specs=[pl.BlockSpec(memory_space=pltpu.SMEM)] + [WHOLE] * 8,
        out_specs=WHOLE,
        out_shape=jax.ShapeDtypeStruct((clips * GROUP, WIDTH), BF16),
        compiler_params=pltpu.CompilerParams(vmem_limit_bytes=24 * MIB),
        cost_estimate=pl.CostEstimate(
            flops=2 * 512 * (704 * 512 + 1024 * 512), bytes_accessed=7 * MIB, transcendentals=0
        ),
        name="handoff",
    )(seq, pos, own, own_a, own_b, bias, gain, weight, peer)


def slot_labels(got_ref):
    slots = got_ref.shape[0]
    clips = slots // GROUP
    head = got_ref[:, :128].astype(F32).reshape(clips, GROUP, 128)
    codes = jnp.sum(jnp.where(iota(head.shape, 1) == LABEL_ROW, head, 0.0), axis=1)
    lane, place = iota((128, slots), 0), iota((128, slots), 1) % GROUP
    spread = jnp.where(lane == place, 32.0, 0.0) + jnp.where(lane == place + 16, 1.0, 0.0)
    by_clip = dot(codes.astype(BF16), spread.astype(BF16))
    mine = iota((clips, slots), 0) == iota((clips, slots), 1) // GROUP
    return jnp.sum(jnp.where(mine, by_clip, 0.0), axis=0, keepdims=True)


def stream_tile(half, first, count, got_ref, label_row, mask, parts):
    slots = got_ref.shape[0]
    want = (iota((count, slots), 0) + (first + 1)).astype(F32)
    place = (want == label_row).astype(F32)
    seen = jnp.sum(place, axis=1, keepdims=True)
    placed = dot(place.astype(BF16), got_ref[...])
    sin_a, cos_a, sin_b, cos_b = parts
    blocks = count // 32
    start = pl.multiple_of(half * (SPAN // 32) + first // 32, 8)
    coarse_sin = sin_a[pl.ds(start, blocks), :].reshape(blocks, 1, WIDTH)
    coarse_cos = cos_a[pl.ds(start, blocks), :].reshape(blocks, 1, WIDTH)
    table = coarse_sin * cos_b[...][None] + coarse_cos * sin_b[...][None]
    return placed + (1.0 - seen) * mask + table.reshape(count, WIDTH)


QKV_TILE = 512


def qkv_kernel(seq_ref, got_ref, sin_a, cos_a, sin_b, cos_b, mask_ref, gain_ref, weight_ref,
               bias_ref, stream_ref, query_ref, key_ref, value_ref):
    label_row = slot_labels(got_ref)
    scale = HEAD_D ** (-0.5) * math.log2(math.e)
    for first in range(0, SPAN, QKV_TILE):
        rows = pl.ds(first, QKV_TILE)
        stream = stream_tile(
            seq_ref[0], first, QKV_TILE, got_ref, label_row, mask_ref[...],
            (sin_a, cos_a, sin_b, cos_b),
        )
        stream_ref[rows, :] = stream
        normed = norm(stream, gain_ref[0:1, :]).astype(BF16)
        out = dot(normed, weight_ref[...]) + bias_ref[...]
        query_ref[rows, :] = (out[:, :WIDTH] * scale).astype(BF16)
        key_ref[rows, :] = out[:, WIDTH : 2 * WIDTH].astype(BF16)
        value_ref[:, rows] = out[:, 2 * WIDTH :].T.astype(BF16)


def own_qkv(seq, got, parts, mask, gain, weight, bias):
    return pl.pallas_call(
        qkv_kernel,
        in_specs=[pl.BlockSpec(memory_space=pltpu.SMEM)] + [WHOLE] * 9,
        out_specs=[WHOLE] * 4,
        out_shape=[
            jax.ShapeDtypeStruct((SPAN, WIDTH), F32),
            jax.ShapeDtypeStruct((SPAN, WIDTH), BF16),
            jax.ShapeDtypeStruct((SPAN, WIDTH), BF16),
            jax.ShapeDtypeStruct((WIDTH, SPAN), BF16),
        ],
        compiler_params=pltpu.CompilerParams(vmem_limit_bytes=20 * MIB),
        cost_estimate=pl.CostEstimate(
            flops=2 * SPAN * WIDTH * (3 * WIDTH + SPAN), bytes_accessed=9 * MIB, transcendentals=0
        ),
        name="own_qkv",
    )(seq, got, *parts, mask, gain, weight, bias)


ROW_TILE = 512
FF_TILE = 512


def decoder_kernel(seq_ref, query_ref, key_ref, value_ref, stream_ref, got_ref, sin_a, cos_a,
                   sin_b, cos_b, mask_ref, gain_ref, weight_ref, bias_ref, out_weight_ref,
                   out_bias_ref, fc1_ref, fc1_bias_ref, fc2_ref, fc2_bias_ref, out_ref, peer_key,
                   peer_value, attended, hidden):
    label_row = slot_labels(got_ref)
    other = 1 - seq_ref[0]
    for first in range(0, SPAN, QKV_TILE):
        rows = pl.ds(first, QKV_TILE)
        stream = stream_tile(
            other, first, QKV_TILE, got_ref, label_row, mask_ref[...],
            (sin_a, cos_a, sin_b, cos_b),
        )
        normed = norm(stream, gain_ref[0:1, :]).astype(BF16)
        out = dot(normed, weight_ref[:, WIDTH:]) + bias_ref[:, WIDTH:]
        peer_key[rows, :] = out[:, :WIDTH].astype(BF16)
        peer_value[:, rows] = out[:, WIDTH:].T.astype(BF16)

    head_of = (iota((WIDTH, 128), 0) // HEAD_D == iota((WIDTH, 128), 1)).astype(F32).astype(BF16)

    def top(ref):
        return jnp.max(dot(ref[...] * ref[...], head_of), axis=0, keepdims=True)

    def largest(ref):
        return jnp.max(jnp.abs(ref[...].astype(F32)))

    score_top = jnp.max(top(query_ref) * jnp.maximum(top(key_ref), top(peer_key)))
    value_top = jnp.maximum(largest(value_ref), largest(peer_value))
    safe = (score_top <= SAFE * SAFE) & (value_top <= SAFE_VALUE)
    halves = ((key_ref, value_ref), (peer_key, peer_value))

    def attend(pair, peaked):
        lanes = pl.ds(pl.multiple_of(pair * 128, 128), 128)
        query = query_ref[:, lanes]
        mixed = []
        for half in range(2):
            own_lane = (iota((1, 128), 1) < HEAD_D) == (half == 0)
            own_row = (iota((128, 1), 0) < HEAD_D) == (half == 0)
            masked = jnp.where(own_lane, query, jnp.zeros_like(query))

            def score(keys):
                return lax.dot_general(
                    keys[:, lanes], masked, (((1,), (1,)), ((), ())), preferred_element_type=F32
                )

            if peaked:
                peak = jnp.maximum(
                    *(jnp.max(score(keys), axis=0, keepdims=True) for keys, _ in halves)
                )
            total = None
            for keys, values in halves:
                scores = score(keys)
                if peaked:
                    scores = scores - peak
                weights = jnp.exp2(scores).astype(BF16)
                value = values[lanes, :]
                value = jnp.where(own_row, value, jnp.ones_like(value))
                part = dot(value, weights)
                total = part if total is None else total + part
            mixed.append(total)
        first = mixed[0][:HEAD_D] / mixed[0][HEAD_D:]
        second = mixed[1][HEAD_D:] / mixed[1][:HEAD_D]
        attended[:, lanes] = jnp.concatenate([first, second], axis=0).T.astype(BF16)

    def all_heads(peaked):
        def one_pair(pair, carry):
            attend(pair, peaked)
            return carry

        lax.fori_loop(0, HEADS // 2, one_pair, 0)

    @pl.when(safe)
    def _():
        all_heads(False)

    @pl.when(jnp.logical_not(safe))
    def _():
        all_heads(True)

    for first in range(0, SPAN, ROW_TILE):
        rows = pl.ds(first, ROW_TILE)
        stream2 = stream_ref[rows, :] + dot(attended[rows, :], out_weight_ref[...]) + out_bias_ref[...]
        normed2 = norm(stream2, gain_ref[1:2, :]).astype(BF16)
        for at in range(0, hidden.shape[1], FF_TILE):
            units = pl.ds(at, FF_TILE)
            inner = dot(normed2, fc1_ref[:, units]) + fc1_bias_ref[:, units]
            hidden[:, units] = gelu(inner).astype(BF16)
        out_ref[rows, :] = (stream2 + dot(hidden[...], fc2_ref[...]) + fc2_bias_ref[...]).astype(BF16)


def decoder(seq, query, key, value, stream, got, parts, mask, gain, weight, bias, out_weight,
            out_bias, fc1, fc1_bias, fc2, fc2_bias):
    tail = (mask, gain, weight, bias, out_weight, out_bias, fc1, fc1_bias, fc2, fc2_bias)
    return pl.pallas_call(
        decoder_kernel,
        in_specs=[pl.BlockSpec(memory_space=pltpu.SMEM)] + [WHOLE] * (5 + len(parts) + len(tail)),
        out_specs=WHOLE,
        out_shape=jax.ShapeDtypeStruct((SPAN, WIDTH), BF16),
        scratch_shapes=[
            pltpu.VMEM((SPAN, WIDTH), BF16),
            pltpu.VMEM((WIDTH, SPAN), BF16),
            pltpu.VMEM((SPAN, WIDTH), BF16),
            pltpu.VMEM((ROW_TILE, fc1.shape[1]), BF16),
        ],
        compiler_params=pltpu.CompilerParams(vmem_limit_bytes=DEC_VMEM * MIB),
        cost_estimate=pl.CostEstimate(
            flops=4 * SPAN * CLIP_LEN * WIDTH + 2 * SPAN * WIDTH * (WIDTH + 4096 + 2048),
            bytes_accessed=16 * MIB,
            transcendentals=HEADS * SPAN * CLIP_LEN,
        ),
        name="decoder",
    )(seq, query, key, value, stream, got, *parts, *tail)


DEC_VMEM = 32


def body(
    enc_rows,
    visible_pos,
    enc_norm_gain,
    enc_fc1,
    enc_fc1_bias,
    enc_fc2,
    enc_fc2_bias,
    handoff_weight,
    mask_token,
    dec_norm_gain,
    qkv_weight,
    qkv_bias,
    out_weight,
    out_bias,
    dec_fc1,
    dec_fc1_bias,
    dec_fc2,
    dec_fc2_bias,
):
    def swap(values):
        return lax.ppermute(values, "seq", [(0, 1), (1, 0)])

    def row(values):
        return values.reshape(1, -1)

    clips = lax.axis_size("rows")
    seq = lax.axis_index("seq").astype(jnp.int32).reshape(1)
    parts = tuple(jnp.asarray(part) for part in sinusoid_parts())
    bias1, bias2 = row(enc_fc1_bias), row(enc_fc2_bias)
    peer_rows = swap(enc_rows)
    peer_pos = swap(visible_pos)
    own_part, fc1_here, fc2_here = first_encoder_mlp(enc_rows, enc_norm_gain, enc_fc1, bias1, enc_fc2)
    peer_rows, peer_pos, own_part = lax.optimization_barrier((peer_rows, peer_pos, own_part))
    peer_part = second_encoder_mlp(peer_rows, enc_norm_gain, fc1_here, bias1, fc2_here)
    pos = jnp.concatenate([visible_pos, peer_pos]).reshape(1, -1)
    peer = projection(peer_rows, peer_part, swap(own_part), bias2, enc_norm_gain, handoff_weight)
    payload = handoff(
        seq, pos, enc_rows, own_part, swap(peer_part), bias2, enc_norm_gain, handoff_weight, peer, clips
    )
    got = lax.all_to_all(
        payload.reshape(clips, GROUP, WIDTH), "rows", split_axis=0, concat_axis=0, tiled=True
    ).reshape(clips * GROUP, WIDTH)
    mask = row(mask_token)
    qkv_bias = row(qkv_bias)
    peer_got = swap(got)
    stream, query, key, value = own_qkv(
        seq, got, parts, mask, dec_norm_gain, qkv_weight, qkv_bias
    )
    decoded = decoder(
        seq, query, key, value, stream, peer_got, parts, mask, dec_norm_gain, qkv_weight, qkv_bias,
        out_weight, row(out_bias), dec_fc1, row(dec_fc1_bias), dec_fc2, row(dec_fc2_bias),
    )
    return decoded.reshape(1, SPAN, WIDTH)


def solution(mesh):
    return jax.shard_map(
        body,
        mesh=mesh,
        in_specs=(
            P(("rows", "seq"), None),
            P(("rows", "seq")),
            P(),
            P(None, "seq"),
            P("seq"),
            P("seq", None),
            P(),
            P(),
            P(),
            P(),
            P(),
            P(),
            P(),
            P(),
            P(),
            P(),
            P(),
            P(),
        ),
        out_specs=P("rows", "seq", None),
        check_vma=False,
    )
```

```python
import math

import jax
import jax.numpy as jnp
import numpy as np
from jax import lax
from jax.experimental import pallas as pl
from jax.experimental.pallas import tpu as pltpu
from jax.sharding import PartitionSpec as P

HEADS = 8
CLIP_LEN = 2048
SPAN = 1024
WIDTH = 512
HEAD_D = 64
GROUP = 16
LABEL_ROW = 12
EPS = 1e-06
F32 = jnp.float32
BF16 = jnp.bfloat16
MIB = 1 << 20
WHOLE = pl.BlockSpec(memory_space=pltpu.VMEM)
SAFE = 60.0
SAFE_VALUE = 2.0**40

def norm(values, gain):
    mean = jnp.mean(values, axis=-1, keepdims=True)
    centered = values - mean
    spread = jnp.mean(centered * centered, axis=-1, keepdims=True)
    return centered * lax.rsqrt(spread + EPS) * gain


def gelu(x):
    half = 0.5 * x
    return half + half * lax.erf(x * (0.5**0.5))


def dot(a, b):
    return jnp.dot(a, b, preferred_element_type=F32)


def iota(shape, dim):
    return lax.broadcasted_iota(jnp.int32, shape, dim)


def sinusoid_parts():
    column = np.arange(WIDTH)
    rate = 10000.0 ** (-(2 * (column // 2)) / WIDTH)
    phase = np.where(column % 2 == 0, 0.0, np.pi / 2)
    coarse = 32.0 * np.arange(CLIP_LEN // 32)[:, None] * rate[None, :] + phase[None, :]
    fine = np.arange(32)[:, None] * rate[None, :]
    return tuple(
        np.asarray(part, np.float32)
        for part in (np.sin(coarse), np.cos(coarse), np.sin(fine), np.cos(fine))
    )


ENC_TILE = 512
IN_FLIGHT = 2
IN_SIZES = (1024, 2048)
OUT_SIZES = (1408,)


def tiles_of(sizes):
    starts = [sum(sizes[:i]) for i in range(len(sizes))]
    return [(start, start + size) for start, size in zip(starts, sizes)]


def cut(start, stop):
    return [pl.ds(at, min(ENC_TILE, stop - at)) for at in range(start, stop, ENC_TILE)]


def enc_kernel(rows_ref, gain_ref, w1_ref, b1_ref, w2_ref, out_ref, w1, w2, rows, gain, b1, hidden,
               arrived, arrived1, arrived2):
    small = [
        pltpu.make_async_copy(source, target, arrived.at[i])
        for i, (source, target) in enumerate(((rows_ref, rows), (gain_ref, gain), (b1_ref, b1)))
    ]
    loads = []
    for sizes, source, target, sems in ((IN_SIZES, w1_ref, w1, arrived1), (OUT_SIZES, w2_ref, w2, arrived2)):
        for i, (start, stop) in enumerate(tiles_of(sizes)):
            tile = pl.ds(start, stop - start)
            loads.append(pltpu.make_async_copy(source.at[:, tile], target.at[:, tile], sems.at[i]))
    for load in small + loads[:IN_FLIGHT]:
        load.start()

    def take(i):
        loads[i].wait()
        if i + IN_FLIGHT < len(loads):
            loads[i + IN_FLIGHT].start()

    for load in small:
        load.wait()
    normed = norm(rows[...].astype(F32), gain[0:1, :]).astype(BF16)
    for i, (start, stop) in enumerate(tiles_of(IN_SIZES)):
        take(i)
        for tile in cut(start, stop):
            hidden[:, tile] = gelu(dot(normed, w1[:, tile]) + b1[:, tile]).astype(BF16)
    for i, (start, stop) in enumerate(tiles_of(OUT_SIZES)):
        take(len(IN_SIZES) + i)
        for tile in cut(start, stop):
            out_ref[:, tile] = dot(hidden[...], w2[:, tile]).astype(BF16)


def enc_cost(count, width, units):
    return pl.CostEstimate(
        flops=4 * count * width * units,
        bytes_accessed=4 * width * units + 4 * count * width,
        transcendentals=count * units,
    )


def first_encoder_mlp(rows, gain, w1, b1, w2):
    count, width = rows.shape
    units = w1.shape[1]
    far = pl.BlockSpec(memory_space=pl.ANY)
    return pl.pallas_call(
        enc_kernel,
        in_specs=[far] * 5,
        out_specs=[WHOLE] * 3,
        out_shape=[
            jax.ShapeDtypeStruct((count, width), BF16),
            jax.ShapeDtypeStruct(w1.shape, BF16),
            jax.ShapeDtypeStruct(w2.shape, BF16),
        ],
        scratch_shapes=[
            pltpu.VMEM((count, width), BF16),
            pltpu.VMEM(gain.shape, F32),
            pltpu.VMEM(b1.shape, F32),
            pltpu.VMEM((count, units), BF16),
            pltpu.SemaphoreType.DMA((3,)),
            pltpu.SemaphoreType.DMA((len(IN_SIZES),)),
            pltpu.SemaphoreType.DMA((len(OUT_SIZES),)),
        ],
        compiler_params=pltpu.CompilerParams(vmem_limit_bytes=FIRST_VMEM),
        cost_estimate=enc_cost(count, width, units),
        name="first_encoder_mlp",
    )(rows, gain, w1, b1, w2)


def second_enc_kernel(rows_ref, gain_ref, w1, b1, w2, out_ref, hidden):
    units, width = w2.shape
    normed = norm(rows_ref[...].astype(F32), gain_ref[0:1, :]).astype(BF16)
    for tile in cut(0, units):
        hidden[:, tile] = gelu(dot(normed, w1[:, tile]) + b1[:, tile]).astype(BF16)
    for tile in cut(0, width):
        out_ref[:, tile] = dot(hidden[...], w2[:, tile]).astype(BF16)


def second_encoder_mlp(rows, gain, w1, b1, w2):
    count, width = rows.shape
    units = w1.shape[1]
    return pl.pallas_call(
        second_enc_kernel,
        in_specs=[WHOLE] * 5,
        out_specs=WHOLE,
        out_shape=jax.ShapeDtypeStruct((count, width), BF16),
        scratch_shapes=[pltpu.VMEM((count, units), BF16)],
        compiler_params=pltpu.CompilerParams(vmem_limit_bytes=ENC_VMEM * MIB),
        cost_estimate=enc_cost(count, width, units),
        name="second_encoder_mlp",
    )(rows, gain, w1, b1, w2)
ENC_VMEM = 16
FIRST_VMEM = 34 * MIB


def project(rows, part_a, part_b, bias_ref, gain_ref, weight_ref):
    encoded = (
        rows[...].astype(F32) + (part_a[...].astype(F32) + part_b[...].astype(F32)) + bias_ref[...]
    )
    final = norm(encoded, gain_ref[1:2, :]).astype(BF16)
    return dot(final, weight_ref[...]).astype(BF16)


def project_kernel(rows, part_a, part_b, bias_ref, gain_ref, weight_ref, out_ref):
    out_ref[...] = project(rows, part_a, part_b, bias_ref, gain_ref, weight_ref)


def projection(rows, part_a, part_b, bias, gain, weight):
    return pl.pallas_call(
        project_kernel,
        in_specs=[WHOLE] * 6,
        out_specs=WHOLE,
        out_shape=jax.ShapeDtypeStruct((rows.shape[0], WIDTH), BF16),
        compiler_params=pltpu.CompilerParams(vmem_limit_bytes=16 * MIB),
        cost_estimate=pl.CostEstimate(
            flops=2 * rows.size * WIDTH, bytes_accessed=4 * MIB, transcendentals=0
        ),
        name="projection",
    )(rows, part_a, part_b, bias, gain, weight)


def handoff_kernel(seq_ref, pos_ref, own_ref, own_a, own_b, bias_ref, gain_ref, weight_ref,
                   peer_ref, out_ref):
    tokens = pos_ref.shape[1]
    own = project(own_ref, own_a, own_b, bias_ref, gain_ref, weight_ref)
    projected = jnp.concatenate([own, peer_ref[...]], axis=0)
    pos = pos_ref[...]
    chosen = ((pos >> 10) & 1) == seq_ref[0]
    clip_row = jnp.where(chosen, pos >> 11, -1).astype(F32)
    label_row = ((pos & (SPAN - 1)) + 1).astype(F32)
    down, across = iota((tokens, tokens), 0), iota((tokens, tokens), 1)
    same = down == across
    clip_col = jnp.sum(jnp.where(same, clip_row, 0.0), axis=1, keepdims=True)
    label_col = jnp.sum(jnp.where(same, label_row, 0.0), axis=1, keepdims=True)
    alike = clip_col == clip_row
    rank_col = jnp.sum(jnp.where(alike & (across < down), 1.0, 0.0), axis=1, keepdims=True)
    rank_row = jnp.sum(jnp.where(alike & (down < across), 1.0, 0.0), axis=0, keepdims=True)
    clips = out_ref.shape[0] // GROUP
    slot_row = jnp.where(clip_row >= 0, clip_row * GROUP + rank_row, -1.0).astype(jnp.int32)
    pick = (iota((clips * GROUP, tokens), 0) == slot_row).astype(F32).astype(BF16)
    packed = dot(pick, projected).astype(BF16).reshape(clips, GROUP, WIDTH)
    to_clip = (iota((clips, tokens), 0) == clip_row.astype(jnp.int32)).astype(F32).astype(BF16)
    upper = jnp.floor(label_col * (1.0 / 32.0))
    lower = label_col - 32.0 * upper
    lane = iota((tokens, 128), 1).astype(F32)
    codes = jnp.where(lane == rank_col, upper, 0.0) + jnp.where(lane == rank_col + 16.0, lower, 0.0)
    labels = dot(to_clip, codes.astype(BF16))
    first = jnp.where(
        iota((clips, GROUP, 128), 1) == LABEL_ROW,
        labels.reshape(clips, 1, 128),
        packed[:, :, :128].astype(F32),
    ).astype(BF16)
    out_ref[:, :128] = first.reshape(clips * GROUP, 128)
    out_ref[:, 128:] = packed[:, :, 128:].reshape(clips * GROUP, WIDTH - 128)


def handoff(seq, pos, own, own_a, own_b, bias, gain, weight, peer, clips):
    return pl.pallas_call(
        handoff_kernel,
        in_specs=[pl.BlockSpec(memory_space=pltpu.SMEM)] + [WHOLE] * 8,
        out_specs=WHOLE,
        out_shape=jax.ShapeDtypeStruct((clips * GROUP, WIDTH), BF16),
        compiler_params=pltpu.CompilerParams(vmem_limit_bytes=24 * MIB),
        cost_estimate=pl.CostEstimate(
            flops=2 * 512 * (704 * 512 + 1024 * 512), bytes_accessed=7 * MIB, transcendentals=0
        ),
        name="handoff",
    )(seq, pos, own, own_a, own_b, bias, gain, weight, peer)


def slot_labels(got_ref):
    slots = got_ref.shape[0]
    clips = slots // GROUP
    head = got_ref[:, :128].astype(F32).reshape(clips, GROUP, 128)
    codes = jnp.sum(jnp.where(iota(head.shape, 1) == LABEL_ROW, head, 0.0), axis=1)
    lane, place = iota((128, slots), 0), iota((128, slots), 1) % GROUP
    spread = jnp.where(lane == place, 32.0, 0.0) + jnp.where(lane == place + 16, 1.0, 0.0)
    by_clip = dot(codes.astype(BF16), spread.astype(BF16))
    mine = iota((clips, slots), 0) == iota((clips, slots), 1) // GROUP
    return jnp.sum(jnp.where(mine, by_clip, 0.0), axis=0, keepdims=True)


def stream_tile(half, first, count, got_ref, label_row, mask, parts):
    slots = got_ref.shape[0]
    want = (iota((count, slots), 0) + (first + 1)).astype(F32)
    place = (want == label_row).astype(F32)
    seen = jnp.sum(place, axis=1, keepdims=True)
    placed = dot(place.astype(BF16), got_ref[...])
    sin_a, cos_a, sin_b, cos_b = parts
    blocks = count // 32
    start = pl.multiple_of(half * (SPAN // 32) + first // 32, 8)
    coarse_sin = sin_a[pl.ds(start, blocks), :].reshape(blocks, 1, WIDTH)
    coarse_cos = cos_a[pl.ds(start, blocks), :].reshape(blocks, 1, WIDTH)
    table = coarse_sin * cos_b[...][None] + coarse_cos * sin_b[...][None]
    return placed + (1.0 - seen) * mask + table.reshape(count, WIDTH)


QKV_TILE = 512


def qkv_kernel(seq_ref, got_ref, sin_a, cos_a, sin_b, cos_b, mask_ref, gain_ref, weight_ref,
               bias_ref, stream_ref, query_ref, key_ref, value_ref):
    label_row = slot_labels(got_ref)
    scale = HEAD_D ** (-0.5) * math.log2(math.e)
    for first in range(0, SPAN, QKV_TILE):
        rows = pl.ds(first, QKV_TILE)
        stream = stream_tile(
            seq_ref[0], first, QKV_TILE, got_ref, label_row, mask_ref[...],
            (sin_a, cos_a, sin_b, cos_b),
        )
        stream_ref[rows, :] = stream
        normed = norm(stream, gain_ref[0:1, :]).astype(BF16)
        out = dot(normed, weight_ref[...]) + bias_ref[...]
        query_ref[rows, :] = (out[:, :WIDTH] * scale).astype(BF16)
        key_ref[rows, :] = out[:, WIDTH : 2 * WIDTH].astype(BF16)
        value_ref[:, rows] = out[:, 2 * WIDTH :].T.astype(BF16)


def own_qkv(seq, got, parts, mask, gain, weight, bias):
    return pl.pallas_call(
        qkv_kernel,
        in_specs=[pl.BlockSpec(memory_space=pltpu.SMEM)] + [WHOLE] * 9,
        out_specs=[WHOLE] * 4,
        out_shape=[
            jax.ShapeDtypeStruct((SPAN, WIDTH), F32),
            jax.ShapeDtypeStruct((SPAN, WIDTH), BF16),
            jax.ShapeDtypeStruct((SPAN, WIDTH), BF16),
            jax.ShapeDtypeStruct((WIDTH, SPAN), BF16),
        ],
        compiler_params=pltpu.CompilerParams(vmem_limit_bytes=20 * MIB),
        cost_estimate=pl.CostEstimate(
            flops=2 * SPAN * WIDTH * (3 * WIDTH + SPAN), bytes_accessed=9 * MIB, transcendentals=0
        ),
        name="own_qkv",
    )(seq, got, *parts, mask, gain, weight, bias)


ROW_TILE = 1024
FF_TILE = 512


def top(ref):
    head_of = (iota((WIDTH, 128), 0) // HEAD_D == iota((WIDTH, 128), 1)).astype(F32).astype(BF16)
    return jnp.max(dot(ref[...] * ref[...], head_of), axis=0, keepdims=True)


def is_safe(query_top, key_ref, value_ref):
    score_top = jnp.max(query_top * top(key_ref))
    value_top = jnp.max(jnp.abs(value_ref[...].astype(F32)))
    return (score_top <= SAFE * SAFE) & (value_top <= SAFE_VALUE)


def head_scores(query_ref, key_ref, pair, half):
    lanes = pl.ds(pl.multiple_of(pair * 128, 128), 128)
    query = query_ref[:, lanes]
    own_lane = (iota((1, 128), 1) < HEAD_D) == (half == 0)
    masked = jnp.where(own_lane, query, jnp.zeros_like(query))
    return lax.dot_general(
        key_ref[:, lanes], masked, (((1,), (1,)), ((), ())), preferred_element_type=F32
    )


def head_total(value_ref, weights, pair, half):
    value = value_ref[pl.ds(pl.multiple_of(pair * 128, 128), 128), :]
    own_row = (iota((128, 1), 0) < HEAD_D) == (half == 0)
    return dot(jnp.where(own_row, value, jnp.ones_like(value)), weights.astype(BF16))


def for_all_pairs(safe, attend):
    def run(peaked):
        def one_pair(pair, carry):
            attend(pair, peaked)
            return carry

        lax.fori_loop(0, HEADS // 2, one_pair, 0, unroll=1 if peaked else HEADS // 2)

    pl.when(safe)(lambda: run(False))
    pl.when(jnp.logical_not(safe))(lambda: run(True))


def own_attention_kernel(query_ref, key_ref, value_ref, total_ref, shift_ref, top_ref, safe_ref):
    query_top = top(query_ref)
    top_ref[...] = query_top
    safe = is_safe(query_top, key_ref, value_ref)
    safe_ref[0] = safe.astype(jnp.int32)

    def attend(pair, peaked):
        for half in range(2):
            head = 2 * pair + half
            scores = head_scores(query_ref, key_ref, pair, half)
            if peaked:
                peak = jnp.max(scores, axis=0, keepdims=True)
                scores = scores - peak
                shift_ref[head] = peak
            else:
                shift_ref[head] = jnp.zeros((1, SPAN), F32)
            total_ref[head] = head_total(value_ref, jnp.exp2(scores), pair, half)

    for_all_pairs(safe, attend)


def own_attention(query, key, value):
    return pl.pallas_call(
        own_attention_kernel,
        in_specs=[WHOLE] * 3,
        out_specs=[WHOLE] * 3 + [pl.BlockSpec(memory_space=pltpu.SMEM)],
        out_shape=[
            jax.ShapeDtypeStruct((HEADS, 128, SPAN), F32),
            jax.ShapeDtypeStruct((HEADS, 1, SPAN), F32),
            jax.ShapeDtypeStruct((1, 128), F32),
            jax.ShapeDtypeStruct((1,), jnp.int32),
        ],
        compiler_params=pltpu.CompilerParams(vmem_limit_bytes=DEC_VMEM * MIB),
        cost_estimate=pl.CostEstimate(
            flops=16 * SPAN * SPAN * WIDTH,
            bytes_accessed=8 * MIB,
            transcendentals=HEADS * SPAN * SPAN,
        ),
        name="own_attention",
    )(query, key, value)


def decoder_kernel(safe_ref, query_ref, key_ref, value_ref, total_ref, shift_ref, top_ref,
                   stream_ref, gain_ref, out_weight_ref, out_bias_ref, fc1_ref, fc1_bias_ref,
                   fc2_ref, fc2_bias_ref, out_ref, attended, hidden):
    safe = (safe_ref[0] == 1) & is_safe(top_ref[...], key_ref, value_ref)

    def attend(pair, peaked):
        mixed = []
        for half in range(2):
            head = 2 * pair + half
            scores = head_scores(query_ref, key_ref, pair, half)
            before = total_ref[head]
            if peaked:
                shift = shift_ref[head]
                peak = jnp.maximum(shift, jnp.max(scores, axis=0, keepdims=True))
                scores = scores - peak
                before = before * jnp.exp2(shift - peak)
            mixed.append(before + head_total(value_ref, jnp.exp2(scores), pair, half))
        first = mixed[0][:HEAD_D] / mixed[0][HEAD_D:]
        second = mixed[1][HEAD_D:] / mixed[1][:HEAD_D]
        lanes = pl.ds(pl.multiple_of(pair * 128, 128), 128)
        attended[:, lanes] = jnp.concatenate([first, second], axis=0).T.astype(BF16)

    for_all_pairs(safe, attend)

    for first in range(0, SPAN, ROW_TILE):
        rows = pl.ds(first, ROW_TILE)
        stream2 = stream_ref[rows, :] + dot(attended[rows, :], out_weight_ref[...]) + out_bias_ref[...]
        normed2 = norm(stream2, gain_ref[1:2, :]).astype(BF16)
        for at in range(0, hidden.shape[1], FF_TILE):
            units = pl.ds(at, FF_TILE)
            inner = dot(normed2, fc1_ref[:, units]) + fc1_bias_ref[:, units]
            hidden[:, units] = gelu(inner).astype(BF16)
        out_ref[rows, :] = (stream2 + dot(hidden[...], fc2_ref[...]) + fc2_bias_ref[...]).astype(BF16)


def decoder(safe, *rest):
    fc1 = rest[-4]
    return pl.pallas_call(
        decoder_kernel,
        in_specs=[pl.BlockSpec(memory_space=pltpu.SMEM)] + [WHOLE] * len(rest),
        out_specs=WHOLE,
        out_shape=jax.ShapeDtypeStruct((SPAN, WIDTH), BF16),
        scratch_shapes=[
            pltpu.VMEM((SPAN, WIDTH), BF16),
            pltpu.VMEM((ROW_TILE, fc1.shape[1]), BF16),
        ],
        compiler_params=pltpu.CompilerParams(vmem_limit_bytes=DEC_VMEM * MIB),
        cost_estimate=pl.CostEstimate(
            flops=16 * SPAN * SPAN * WIDTH + 2 * SPAN * WIDTH * (WIDTH + 4096),
            bytes_accessed=16 * MIB,
            transcendentals=HEADS * SPAN * SPAN,
        ),
        name="decoder",
    )(safe, *rest)


DEC_VMEM = 32


def body(
    enc_rows,
    visible_pos,
    enc_norm_gain,
    enc_fc1,
    enc_fc1_bias,
    enc_fc2,
    enc_fc2_bias,
    handoff_weight,
    mask_token,
    dec_norm_gain,
    qkv_weight,
    qkv_bias,
    out_weight,
    out_bias,
    dec_fc1,
    dec_fc1_bias,
    dec_fc2,
    dec_fc2_bias,
):
    def swap(values):
        return lax.ppermute(values, "seq", [(0, 1), (1, 0)])

    def row(values):
        return values.reshape(1, -1)

    clips = lax.axis_size("rows")
    seq = lax.axis_index("seq").astype(jnp.int32).reshape(1)
    parts = tuple(jnp.asarray(part) for part in sinusoid_parts())
    bias1, bias2 = row(enc_fc1_bias), row(enc_fc2_bias)
    peer_rows = swap(enc_rows)
    peer_pos = swap(visible_pos)
    own_part, fc1_here, fc2_here = first_encoder_mlp(enc_rows, enc_norm_gain, enc_fc1, bias1, enc_fc2)
    peer_rows, peer_pos, own_part = lax.optimization_barrier((peer_rows, peer_pos, own_part))
    peer_part = second_encoder_mlp(peer_rows, enc_norm_gain, fc1_here, bias1, fc2_here)
    pos = jnp.concatenate([visible_pos, peer_pos]).reshape(1, -1)
    peer = projection(peer_rows, peer_part, swap(own_part), bias2, enc_norm_gain, handoff_weight)
    payload = handoff(
        seq, pos, enc_rows, own_part, swap(peer_part), bias2, enc_norm_gain, handoff_weight, peer, clips
    )
    got = lax.all_to_all(
        payload.reshape(clips, GROUP, WIDTH), "rows", split_axis=0, concat_axis=0, tiled=True
    ).reshape(clips * GROUP, WIDTH)
    mask = row(mask_token)
    qkv_bias = row(qkv_bias)
    stream, query, key, value = own_qkv(
        seq, got, parts, mask, dec_norm_gain, qkv_weight, qkv_bias
    )
    peer_key, peer_value = swap(key), swap(value)
    total, shift, query_top, safe = own_attention(query, key, value)
    decoded = decoder(
        safe, query, peer_key, peer_value, total, shift, query_top, stream, dec_norm_gain,
        out_weight, row(out_bias), dec_fc1, row(dec_fc1_bias), dec_fc2, row(dec_fc2_bias),
    )
    return decoded.reshape(1, SPAN, WIDTH)


def solution(mesh):
    return jax.shard_map(
        body,
        mesh=mesh,
        in_specs=(
            P(("rows", "seq"), None),
            P(("rows", "seq")),
            P(),
            P(None, "seq"),
            P("seq"),
            P("seq", None),
            P(),
            P(),
            P(),
            P(),
            P(),
            P(),
            P(),
            P(),
            P(),
            P(),
            P(),
            P(),
        ),
        out_specs=P("rows", "seq", None),
        check_vma=False,
    )
```

```python
import math

import jax
import jax.numpy as jnp
import numpy as np
from jax import lax
from jax.experimental import pallas as pl
from jax.experimental.pallas import tpu as pltpu
from jax.sharding import PartitionSpec as P

HEADS = 8
CLIP_LEN = 2048
SPAN = 1024
WIDTH = 512
HEAD_D = 64
GROUP = 16
LABEL_ROW = 12
EPS = 1e-06
F32 = jnp.float32
BF16 = jnp.bfloat16
MIB = 1 << 20
WHOLE = pl.BlockSpec(memory_space=pltpu.VMEM)
SAFE = 60.0
SAFE_VALUE = 2.0**40

def norm(values, gain):
    mean = jnp.mean(values, axis=-1, keepdims=True)
    centered = values - mean
    spread = jnp.mean(centered * centered, axis=-1, keepdims=True)
    return centered * lax.rsqrt(spread + EPS) * gain


def gelu(x):
    half = 0.5 * x
    return half + half * lax.erf(x * (0.5**0.5))


def dot(a, b):
    return jnp.dot(a, b, preferred_element_type=F32)


def iota(shape, dim):
    return lax.broadcasted_iota(jnp.int32, shape, dim)


def sinusoid_parts():
    column = np.arange(WIDTH)
    rate = 10000.0 ** (-(2 * (column // 2)) / WIDTH)
    phase = np.where(column % 2 == 0, 0.0, np.pi / 2)
    coarse = 32.0 * np.arange(CLIP_LEN // 32)[:, None] * rate[None, :] + phase[None, :]
    fine = np.arange(32)[:, None] * rate[None, :]
    return tuple(
        np.asarray(part, np.float32)
        for part in (np.sin(coarse), np.cos(coarse), np.sin(fine), np.cos(fine))
    )


ENC_TILE = 512
IN_FLIGHT = 2
IN_SIZES = (1024, 2048)
OUT_SIZES = (1408,)


def tiles_of(sizes):
    starts = [sum(sizes[:i]) for i in range(len(sizes))]
    return [(start, start + size) for start, size in zip(starts, sizes)]


def cut(start, stop):
    return [pl.ds(at, min(ENC_TILE, stop - at)) for at in range(start, stop, ENC_TILE)]


def enc_kernel(rows_ref, gain_ref, w1_ref, b1_ref, w2_ref, out_ref, w1, w2, rows, gain, b1, hidden,
               arrived, arrived1, arrived2):
    small = [
        pltpu.make_async_copy(source, target, arrived.at[i])
        for i, (source, target) in enumerate(((rows_ref, rows), (gain_ref, gain), (b1_ref, b1)))
    ]
    loads = []
    for sizes, source, target, sems in ((IN_SIZES, w1_ref, w1, arrived1), (OUT_SIZES, w2_ref, w2, arrived2)):
        for i, (start, stop) in enumerate(tiles_of(sizes)):
            tile = pl.ds(start, stop - start)
            loads.append(pltpu.make_async_copy(source.at[:, tile], target.at[:, tile], sems.at[i]))
    for load in small + loads[:IN_FLIGHT]:
        load.start()

    def take(i):
        loads[i].wait()
        if i + IN_FLIGHT < len(loads):
            loads[i + IN_FLIGHT].start()

    for load in small:
        load.wait()
    normed = norm(rows[...].astype(F32), gain[0:1, :]).astype(BF16)
    for i, (start, stop) in enumerate(tiles_of(IN_SIZES)):
        take(i)
        for tile in cut(start, stop):
            hidden[:, tile] = gelu(dot(normed, w1[:, tile]) + b1[:, tile]).astype(BF16)
    for i, (start, stop) in enumerate(tiles_of(OUT_SIZES)):
        take(len(IN_SIZES) + i)
        for tile in cut(start, stop):
            out_ref[:, tile] = dot(hidden[...], w2[:, tile]).astype(BF16)


def enc_cost(count, width, units):
    return pl.CostEstimate(
        flops=4 * count * width * units,
        bytes_accessed=4 * width * units + 4 * count * width,
        transcendentals=count * units,
    )


def first_encoder_mlp(rows, gain, w1, b1, w2):
    count, width = rows.shape
    units = w1.shape[1]
    far = pl.BlockSpec(memory_space=pl.ANY)
    return pl.pallas_call(
        enc_kernel,
        in_specs=[far] * 5,
        out_specs=[WHOLE] * 3,
        out_shape=[
            jax.ShapeDtypeStruct((count, width), BF16),
            jax.ShapeDtypeStruct(w1.shape, BF16),
            jax.ShapeDtypeStruct(w2.shape, BF16),
        ],
        scratch_shapes=[
            pltpu.VMEM((count, width), BF16),
            pltpu.VMEM(gain.shape, F32),
            pltpu.VMEM(b1.shape, F32),
            pltpu.VMEM((count, units), BF16),
            pltpu.SemaphoreType.DMA((3,)),
            pltpu.SemaphoreType.DMA((len(IN_SIZES),)),
            pltpu.SemaphoreType.DMA((len(OUT_SIZES),)),
        ],
        compiler_params=pltpu.CompilerParams(vmem_limit_bytes=FIRST_VMEM),
        cost_estimate=enc_cost(count, width, units),
        name="first_encoder_mlp",
    )(rows, gain, w1, b1, w2)


def second_enc_kernel(rows_ref, gain_ref, w1, b1, w2, out_ref, hidden):
    units, width = w2.shape
    normed = norm(rows_ref[...].astype(F32), gain_ref[0:1, :]).astype(BF16)
    for tile in cut(0, units):
        hidden[:, tile] = gelu(dot(normed, w1[:, tile]) + b1[:, tile]).astype(BF16)
    for tile in cut(0, width):
        out_ref[:, tile] = dot(hidden[...], w2[:, tile]).astype(BF16)


def second_encoder_mlp(rows, gain, w1, b1, w2):
    count, width = rows.shape
    units = w1.shape[1]
    return pl.pallas_call(
        second_enc_kernel,
        in_specs=[WHOLE] * 5,
        out_specs=WHOLE,
        out_shape=jax.ShapeDtypeStruct((count, width), BF16),
        scratch_shapes=[pltpu.VMEM((count, units), BF16)],
        compiler_params=pltpu.CompilerParams(vmem_limit_bytes=ENC_VMEM * MIB),
        cost_estimate=enc_cost(count, width, units),
        name="second_encoder_mlp",
    )(rows, gain, w1, b1, w2)
ENC_VMEM = 16
FIRST_VMEM = 34 * MIB


def project(rows, part_a, part_b, bias_ref, gain_ref, weight_ref):
    encoded = (
        rows[...].astype(F32) + (part_a[...].astype(F32) + part_b[...].astype(F32)) + bias_ref[...]
    )
    final = norm(encoded, gain_ref[1:2, :]).astype(BF16)
    return dot(final, weight_ref[...]).astype(BF16)


def project_kernel(rows, part_a, part_b, bias_ref, gain_ref, weight_ref, out_ref):
    out_ref[...] = project(rows, part_a, part_b, bias_ref, gain_ref, weight_ref)


def projection(rows, part_a, part_b, bias, gain, weight):
    return pl.pallas_call(
        project_kernel,
        in_specs=[WHOLE] * 6,
        out_specs=WHOLE,
        out_shape=jax.ShapeDtypeStruct((rows.shape[0], WIDTH), BF16),
        compiler_params=pltpu.CompilerParams(vmem_limit_bytes=16 * MIB),
        cost_estimate=pl.CostEstimate(
            flops=2 * rows.size * WIDTH, bytes_accessed=4 * MIB, transcendentals=0
        ),
        name="projection",
    )(rows, part_a, part_b, bias, gain, weight)


def handoff_kernel(seq_ref, pos_ref, own_ref, own_a, own_b, bias_ref, gain_ref, weight_ref,
                   peer_ref, out_ref):
    tokens = pos_ref.shape[1]
    own = project(own_ref, own_a, own_b, bias_ref, gain_ref, weight_ref)
    projected = jnp.concatenate([own, peer_ref[...]], axis=0)
    pos = pos_ref[...]
    chosen = ((pos >> 10) & 1) == seq_ref[0]
    clip_row = jnp.where(chosen, pos >> 11, -1).astype(F32)
    label_row = ((pos & (SPAN - 1)) + 1).astype(F32)
    down, across = iota((tokens, tokens), 0), iota((tokens, tokens), 1)
    same = down == across
    clip_col = jnp.sum(jnp.where(same, clip_row, 0.0), axis=1, keepdims=True)
    label_col = jnp.sum(jnp.where(same, label_row, 0.0), axis=1, keepdims=True)
    alike = clip_col == clip_row
    rank_col = jnp.sum(jnp.where(alike & (across < down), 1.0, 0.0), axis=1, keepdims=True)
    rank_row = jnp.sum(jnp.where(alike & (down < across), 1.0, 0.0), axis=0, keepdims=True)
    clips = out_ref.shape[0] // GROUP
    slot_row = jnp.where(clip_row >= 0, clip_row * GROUP + rank_row, -1.0).astype(jnp.int32)
    pick = (iota((clips * GROUP, tokens), 0) == slot_row).astype(F32).astype(BF16)
    packed = dot(pick, projected).astype(BF16).reshape(clips, GROUP, WIDTH)
    to_clip = (iota((clips, tokens), 0) == clip_row.astype(jnp.int32)).astype(F32).astype(BF16)
    upper = jnp.floor(label_col * (1.0 / 32.0))
    lower = label_col - 32.0 * upper
    lane = iota((tokens, 128), 1).astype(F32)
    codes = jnp.where(lane == rank_col, upper, 0.0) + jnp.where(lane == rank_col + 16.0, lower, 0.0)
    labels = dot(to_clip, codes.astype(BF16))
    first = jnp.where(
        iota((clips, GROUP, 128), 1) == LABEL_ROW,
        labels.reshape(clips, 1, 128),
        packed[:, :, :128].astype(F32),
    ).astype(BF16)
    out_ref[:, :128] = first.reshape(clips * GROUP, 128)
    out_ref[:, 128:] = packed[:, :, 128:].reshape(clips * GROUP, WIDTH - 128)


def handoff(seq, pos, own, own_a, own_b, bias, gain, weight, peer, clips):
    return pl.pallas_call(
        handoff_kernel,
        in_specs=[pl.BlockSpec(memory_space=pltpu.SMEM)] + [WHOLE] * 8,
        out_specs=WHOLE,
        out_shape=jax.ShapeDtypeStruct((clips * GROUP, WIDTH), BF16),
        compiler_params=pltpu.CompilerParams(vmem_limit_bytes=24 * MIB),
        cost_estimate=pl.CostEstimate(
            flops=2 * 512 * (704 * 512 + 1024 * 512), bytes_accessed=7 * MIB, transcendentals=0
        ),
        name="handoff",
    )(seq, pos, own, own_a, own_b, bias, gain, weight, peer)


def slot_labels(got_ref):
    slots = got_ref.shape[0]
    clips = slots // GROUP
    head = got_ref[:, :128].astype(F32).reshape(clips, GROUP, 128)
    codes = jnp.sum(jnp.where(iota(head.shape, 1) == LABEL_ROW, head, 0.0), axis=1)
    lane, place = iota((128, slots), 0), iota((128, slots), 1) % GROUP
    spread = jnp.where(lane == place, 32.0, 0.0) + jnp.where(lane == place + 16, 1.0, 0.0)
    by_clip = dot(codes.astype(BF16), spread.astype(BF16))
    mine = iota((clips, slots), 0) == iota((clips, slots), 1) // GROUP
    return jnp.sum(jnp.where(mine, by_clip, 0.0), axis=0, keepdims=True)


def stream_tile(half, first, count, got_ref, label_row, mask, parts):
    slots = got_ref.shape[0]
    want = (iota((count, slots), 0) + (first + 1)).astype(F32)
    place = (want == label_row).astype(F32)
    seen = jnp.sum(place, axis=1, keepdims=True)
    placed = dot(place.astype(BF16), got_ref[...])
    sin_a, cos_a, sin_b, cos_b = parts
    blocks = count // 32
    start = pl.multiple_of(half * (SPAN // 32) + first // 32, 8)
    coarse_sin = sin_a[pl.ds(start, blocks), :].reshape(blocks, 1, WIDTH)
    coarse_cos = cos_a[pl.ds(start, blocks), :].reshape(blocks, 1, WIDTH)
    table = coarse_sin * cos_b[...][None] + coarse_cos * sin_b[...][None]
    return placed + (1.0 - seen) * mask + table.reshape(count, WIDTH)


QKV_TILE = 512


def qkv_kernel(seq_ref, got_ref, sin_a, cos_a, sin_b, cos_b, mask_ref, gain_ref, weight_ref,
               bias_ref, stream_ref, query_ref, key_ref, value_ref):
    label_row = slot_labels(got_ref)
    scale = HEAD_D ** (-0.5) * math.log2(math.e)
    for first in range(0, SPAN, QKV_TILE):
        rows = pl.ds(first, QKV_TILE)
        stream = stream_tile(
            seq_ref[0], first, QKV_TILE, got_ref, label_row, mask_ref[...],
            (sin_a, cos_a, sin_b, cos_b),
        )
        stream_ref[rows, :] = stream
        normed = norm(stream, gain_ref[0:1, :]).astype(BF16)
        out = dot(normed, weight_ref[...]) + bias_ref[...]
        query_ref[rows, :] = (out[:, :WIDTH] * scale).astype(BF16)
        key_ref[rows, :] = out[:, WIDTH : 2 * WIDTH].astype(BF16)
        value_ref[:, rows] = out[:, 2 * WIDTH :].T.astype(BF16)


def own_qkv(seq, got, parts, mask, gain, weight, bias):
    return pl.pallas_call(
        qkv_kernel,
        in_specs=[pl.BlockSpec(memory_space=pltpu.SMEM)] + [WHOLE] * 9,
        out_specs=[WHOLE] * 4,
        out_shape=[
            jax.ShapeDtypeStruct((SPAN, WIDTH), F32),
            jax.ShapeDtypeStruct((SPAN, WIDTH), BF16),
            jax.ShapeDtypeStruct((SPAN, WIDTH), BF16),
            jax.ShapeDtypeStruct((WIDTH, SPAN), BF16),
        ],
        compiler_params=pltpu.CompilerParams(vmem_limit_bytes=20 * MIB),
        cost_estimate=pl.CostEstimate(
            flops=2 * SPAN * WIDTH * (3 * WIDTH + SPAN), bytes_accessed=9 * MIB, transcendentals=0
        ),
        name="own_qkv",
    )(seq, got, *parts, mask, gain, weight, bias)


ROW_TILE = 1024
FF_TILE = 512


def top(ref):
    head_of = (iota((WIDTH, 128), 0) // HEAD_D == iota((WIDTH, 128), 1)).astype(F32).astype(BF16)
    return jnp.max(dot(ref[...] * ref[...], head_of), axis=0, keepdims=True)


def is_safe(query_top, key_ref, value_ref):
    score_top = jnp.max(query_top * top(key_ref))
    value_top = jnp.max(jnp.abs(value_ref[...].astype(F32)))
    return (score_top <= SAFE * SAFE) & (value_top <= SAFE_VALUE)


def head_scores(query_ref, key_ref, pair, half):
    lanes = pl.ds(pl.multiple_of(pair * 128, 128), 128)
    query = query_ref[:, lanes]
    own_lane = (iota((1, 128), 1) < HEAD_D) == (half == 0)
    masked = jnp.where(own_lane, query, jnp.zeros_like(query))
    return lax.dot_general(
        key_ref[:, lanes], masked, (((1,), (1,)), ((), ())), preferred_element_type=F32
    )


def head_total(value_ref, weights, pair, half):
    value = value_ref[pl.ds(pl.multiple_of(pair * 128, 128), 128), :]
    own_row = (iota((128, 1), 0) < HEAD_D) == (half == 0)
    return dot(jnp.where(own_row, value, jnp.ones_like(value)), weights.astype(BF16))


def for_all_pairs(safe, attend):
    def run(peaked):
        def one_pair(pair, carry):
            attend(pair, peaked)
            return carry

        lax.fori_loop(0, HEADS // 2, one_pair, 0, unroll=1 if peaked else HEADS // 2)

    pl.when(safe)(lambda: run(False))
    pl.when(jnp.logical_not(safe))(lambda: run(True))


def own_attention_kernel(query_ref, key_ref, value_ref, total_ref, shift_ref, top_ref, safe_ref):
    query_top = top(query_ref)
    top_ref[...] = query_top
    safe = is_safe(query_top, key_ref, value_ref)
    safe_ref[0] = safe.astype(jnp.int32)

    def attend(pair, peaked):
        for half in range(2):
            head = 2 * pair + half
            scores = head_scores(query_ref, key_ref, pair, half)
            if peaked:
                peak = jnp.max(scores, axis=0, keepdims=True)
                scores = scores - peak
                shift_ref[head] = peak
            else:
                shift_ref[head] = jnp.zeros((1, SPAN), F32)
            total_ref[head] = head_total(value_ref, jnp.exp2(scores), pair, half)

    for_all_pairs(safe, attend)


def own_attention(query, key, value):
    return pl.pallas_call(
        own_attention_kernel,
        in_specs=[WHOLE] * 3,
        out_specs=[WHOLE] * 3 + [pl.BlockSpec(memory_space=pltpu.SMEM)],
        out_shape=[
            jax.ShapeDtypeStruct((HEADS, 128, SPAN), F32),
            jax.ShapeDtypeStruct((HEADS, 1, SPAN), F32),
            jax.ShapeDtypeStruct((1, 128), F32),
            jax.ShapeDtypeStruct((1,), jnp.int32),
        ],
        compiler_params=pltpu.CompilerParams(vmem_limit_bytes=OWN_VMEM * MIB),
        cost_estimate=pl.CostEstimate(
            flops=16 * SPAN * SPAN * WIDTH,
            bytes_accessed=8 * MIB,
            transcendentals=HEADS * SPAN * SPAN,
        ),
        name="own_attention",
    )(query, key, value)


def decoder_kernel(safe_ref, query_ref, key_ref, value_ref, total_ref, shift_ref, top_ref,
                   stream_ref, gain_ref, out_weight_ref, out_bias_ref, fc1_ref, fc1_bias_ref,
                   fc2_ref, fc2_bias_ref, out_ref, attended, hidden):
    safe = (safe_ref[0] == 1) & is_safe(top_ref[...], key_ref, value_ref)

    def attend(pair, peaked):
        mixed = []
        for half in range(2):
            head = 2 * pair + half
            scores = head_scores(query_ref, key_ref, pair, half)
            before = total_ref[head]
            if peaked:
                shift = shift_ref[head]
                peak = jnp.maximum(shift, jnp.max(scores, axis=0, keepdims=True))
                scores = scores - peak
                before = before * jnp.exp2(shift - peak)
            mixed.append(before + head_total(value_ref, jnp.exp2(scores), pair, half))
        first = mixed[0][:HEAD_D] / mixed[0][HEAD_D:]
        second = mixed[1][HEAD_D:] / mixed[1][:HEAD_D]
        lanes = pl.ds(pl.multiple_of(pair * 128, 128), 128)
        attended[:, lanes] = jnp.concatenate([first, second], axis=0).T.astype(BF16)

    for_all_pairs(safe, attend)

    for first in range(0, SPAN, ROW_TILE):
        rows = pl.ds(first, ROW_TILE)
        stream2 = stream_ref[rows, :] + dot(attended[rows, :], out_weight_ref[...]) + out_bias_ref[...]
        normed2 = norm(stream2, gain_ref[1:2, :]).astype(BF16)
        for at in range(0, hidden.shape[1], FF_TILE):
            units = pl.ds(at, FF_TILE)
            inner = dot(normed2, fc1_ref[:, units]) + fc1_bias_ref[:, units]
            hidden[:, units] = gelu(inner).astype(BF16)
        out_ref[rows, :] = (stream2 + dot(hidden[...], fc2_ref[...]) + fc2_bias_ref[...]).astype(BF16)


def decoder(safe, *rest):
    fc1 = rest[-4]
    return pl.pallas_call(
        decoder_kernel,
        in_specs=[pl.BlockSpec(memory_space=pltpu.SMEM)] + [WHOLE] * len(rest),
        out_specs=WHOLE,
        out_shape=jax.ShapeDtypeStruct((SPAN, WIDTH), BF16),
        scratch_shapes=[
            pltpu.VMEM((SPAN, WIDTH), BF16),
            pltpu.VMEM((ROW_TILE, fc1.shape[1]), BF16),
        ],
        compiler_params=pltpu.CompilerParams(vmem_limit_bytes=DEC_VMEM * MIB),
        cost_estimate=pl.CostEstimate(
            flops=16 * SPAN * SPAN * WIDTH + 2 * SPAN * WIDTH * (WIDTH + 4096),
            bytes_accessed=16 * MIB,
            transcendentals=HEADS * SPAN * SPAN,
        ),
        name="decoder",
    )(safe, *rest)


OWN_VMEM = 18
DEC_VMEM = 24


def body(
    enc_rows,
    visible_pos,
    enc_norm_gain,
    enc_fc1,
    enc_fc1_bias,
    enc_fc2,
    enc_fc2_bias,
    handoff_weight,
    mask_token,
    dec_norm_gain,
    qkv_weight,
    qkv_bias,
    out_weight,
    out_bias,
    dec_fc1,
    dec_fc1_bias,
    dec_fc2,
    dec_fc2_bias,
):
    def swap(values):
        return lax.ppermute(values, "seq", [(0, 1), (1, 0)])

    def row(values):
        return values.reshape(1, -1)

    clips = lax.axis_size("rows")
    seq = lax.axis_index("seq").astype(jnp.int32).reshape(1)
    parts = tuple(jnp.asarray(part) for part in sinusoid_parts())
    bias1, bias2 = row(enc_fc1_bias), row(enc_fc2_bias)
    peer_rows = swap(enc_rows)
    peer_pos = swap(visible_pos)
    own_part, fc1_here, fc2_here = first_encoder_mlp(enc_rows, enc_norm_gain, enc_fc1, bias1, enc_fc2)
    peer_rows, peer_pos, own_part = lax.optimization_barrier((peer_rows, peer_pos, own_part))
    peer_part = second_encoder_mlp(peer_rows, enc_norm_gain, fc1_here, bias1, fc2_here)
    pos = jnp.concatenate([visible_pos, peer_pos]).reshape(1, -1)
    peer = projection(peer_rows, peer_part, swap(own_part), bias2, enc_norm_gain, handoff_weight)
    payload = handoff(
        seq, pos, enc_rows, own_part, swap(peer_part), bias2, enc_norm_gain, handoff_weight, peer, clips
    )
    mask, qkv_bias = row(mask_token), row(qkv_bias)
    payload, mask, qkv_bias = lax.optimization_barrier((payload, mask, qkv_bias))
    got = lax.all_to_all(
        payload.reshape(clips, GROUP, WIDTH), "rows", split_axis=0, concat_axis=0, tiled=True
    ).reshape(clips * GROUP, WIDTH)
    stream, query, key, value = own_qkv(
        seq, got, parts, mask, dec_norm_gain, qkv_weight, qkv_bias
    )
    peer_key, peer_value = swap(key), swap(value)
    total, shift, query_top, safe = own_attention(query, key, value)
    decoded = decoder(
        safe, query, peer_key, peer_value, total, shift, query_top, stream, dec_norm_gain,
        out_weight, row(out_bias), dec_fc1, row(dec_fc1_bias), dec_fc2, row(dec_fc2_bias),
    )
    return decoded.reshape(1, SPAN, WIDTH)


def solution(mesh):
    return jax.shard_map(
        body,
        mesh=mesh,
        in_specs=(
            P(("rows", "seq"), None),
            P(("rows", "seq")),
            P(),
            P(None, "seq"),
            P("seq"),
            P("seq", None),
            P(),
            P(),
            P(),
            P(),
            P(),
            P(),
            P(),
            P(),
            P(),
            P(),
            P(),
            P(),
        ),
        out_specs=P("rows", "seq", None),
        check_vma=False,
    )
```

```python
import math

import jax
import jax.numpy as jnp
import numpy as np
from jax import lax
from jax.experimental import pallas as pl
from jax.experimental.pallas import tpu as pltpu
from jax.sharding import PartitionSpec as P

HEADS = 8
CLIP_LEN = 2048
SPAN = 1024
WIDTH = 512
HEAD_D = 64
GROUP = 16
LABEL_ROW = 12
EPS = 1e-06
F32 = jnp.float32
BF16 = jnp.bfloat16
MIB = 1 << 20
WHOLE = pl.BlockSpec(memory_space=pltpu.VMEM)
SAFE = 60.0
SAFE_VALUE = 2.0**40

def norm(values, gain):
    mean = jnp.mean(values, axis=-1, keepdims=True)
    centered = values - mean
    spread = jnp.mean(centered * centered, axis=-1, keepdims=True)
    return centered * lax.rsqrt(spread + EPS) * gain


def gelu(x):
    half = 0.5 * x
    return half + half * lax.erf(x * (0.5**0.5))


def dot(a, b):
    return jnp.dot(a, b, preferred_element_type=F32)


def iota(shape, dim):
    return lax.broadcasted_iota(jnp.int32, shape, dim)


def sinusoid_parts():
    column = np.arange(WIDTH)
    rate = 10000.0 ** (-(2 * (column // 2)) / WIDTH)
    phase = np.where(column % 2 == 0, 0.0, np.pi / 2)
    coarse = 32.0 * np.arange(CLIP_LEN // 32)[:, None] * rate[None, :] + phase[None, :]
    fine = np.arange(32)[:, None] * rate[None, :]
    return tuple(
        np.asarray(part, np.float32)
        for part in (np.sin(coarse), np.cos(coarse), np.sin(fine), np.cos(fine))
    )


ENC_TILE = 512
IN_FLIGHT = 2
IN_SIZES = (1024, 2048)
OUT_SIZES = (1408,)


def tiles_of(sizes):
    starts = [sum(sizes[:i]) for i in range(len(sizes))]
    return [(start, start + size) for start, size in zip(starts, sizes)]


def cut(start, stop):
    return [pl.ds(at, min(ENC_TILE, stop - at)) for at in range(start, stop, ENC_TILE)]


def enc_kernel(rows_ref, gain_ref, w1_ref, b1_ref, w2_ref, out_ref, w1, w2, rows, gain, b1, hidden,
               arrived, arrived1, arrived2):
    small = [
        pltpu.make_async_copy(source, target, arrived.at[i])
        for i, (source, target) in enumerate(((rows_ref, rows), (gain_ref, gain), (b1_ref, b1)))
    ]
    loads = []
    for sizes, source, target, sems in ((IN_SIZES, w1_ref, w1, arrived1), (OUT_SIZES, w2_ref, w2, arrived2)):
        for i, (start, stop) in enumerate(tiles_of(sizes)):
            tile = pl.ds(start, stop - start)
            loads.append(pltpu.make_async_copy(source.at[:, tile], target.at[:, tile], sems.at[i]))
    for load in small + loads[:IN_FLIGHT]:
        load.start()

    def take(i):
        loads[i].wait()
        if i + IN_FLIGHT < len(loads):
            loads[i + IN_FLIGHT].start()

    for load in small:
        load.wait()
    normed = norm(rows[...].astype(F32), gain[0:1, :]).astype(BF16)
    for i, (start, stop) in enumerate(tiles_of(IN_SIZES)):
        take(i)
        for tile in cut(start, stop):
            hidden[:, tile] = gelu(dot(normed, w1[:, tile]) + b1[:, tile]).astype(BF16)
    for i, (start, stop) in enumerate(tiles_of(OUT_SIZES)):
        take(len(IN_SIZES) + i)
        for tile in cut(start, stop):
            out_ref[:, tile] = dot(hidden[...], w2[:, tile]).astype(BF16)


def enc_cost(count, width, units):
    return pl.CostEstimate(
        flops=4 * count * width * units,
        bytes_accessed=4 * width * units + 4 * count * width,
        transcendentals=count * units,
    )


def first_encoder_mlp(rows, gain, w1, b1, w2):
    count, width = rows.shape
    units = w1.shape[1]
    far = pl.BlockSpec(memory_space=pl.ANY)
    return pl.pallas_call(
        enc_kernel,
        in_specs=[far] * 5,
        out_specs=[WHOLE] * 3,
        out_shape=[
            jax.ShapeDtypeStruct((count, width), BF16),
            jax.ShapeDtypeStruct(w1.shape, BF16),
            jax.ShapeDtypeStruct(w2.shape, BF16),
        ],
        scratch_shapes=[
            pltpu.VMEM((count, width), BF16),
            pltpu.VMEM(gain.shape, F32),
            pltpu.VMEM(b1.shape, F32),
            pltpu.VMEM((count, units), BF16),
            pltpu.SemaphoreType.DMA((3,)),
            pltpu.SemaphoreType.DMA((len(IN_SIZES),)),
            pltpu.SemaphoreType.DMA((len(OUT_SIZES),)),
        ],
        compiler_params=pltpu.CompilerParams(vmem_limit_bytes=FIRST_VMEM),
        cost_estimate=enc_cost(count, width, units),
        name="first_encoder_mlp",
    )(rows, gain, w1, b1, w2)


def second_enc_kernel(rows_ref, gain_ref, w1, b1, w2, out_ref, hidden):
    units, width = w2.shape
    normed = norm(rows_ref[...].astype(F32), gain_ref[0:1, :]).astype(BF16)
    for tile in cut(0, units):
        hidden[:, tile] = gelu(dot(normed, w1[:, tile]) + b1[:, tile]).astype(BF16)
    for tile in cut(0, width):
        out_ref[:, tile] = dot(hidden[...], w2[:, tile]).astype(BF16)


def second_encoder_mlp(rows, gain, w1, b1, w2):
    count, width = rows.shape
    units = w1.shape[1]
    return pl.pallas_call(
        second_enc_kernel,
        in_specs=[WHOLE] * 5,
        out_specs=WHOLE,
        out_shape=jax.ShapeDtypeStruct((count, width), BF16),
        scratch_shapes=[pltpu.VMEM((count, units), BF16)],
        compiler_params=pltpu.CompilerParams(vmem_limit_bytes=ENC_VMEM * MIB),
        cost_estimate=enc_cost(count, width, units),
        name="second_encoder_mlp",
    )(rows, gain, w1, b1, w2)
ENC_VMEM = 16
FIRST_VMEM = 34 * MIB


def project(rows, part_a, part_b, bias_ref, gain_ref, weight_ref):
    encoded = (
        rows[...].astype(F32) + (part_a[...].astype(F32) + part_b[...].astype(F32)) + bias_ref[...]
    )
    final = norm(encoded, gain_ref[1:2, :]).astype(BF16)
    return dot(final, weight_ref[...]).astype(BF16)


def project_kernel(rows, part_a, part_b, bias_ref, gain_ref, weight_ref, out_ref):
    out_ref[...] = project(rows, part_a, part_b, bias_ref, gain_ref, weight_ref)


def projection(rows, part_a, part_b, bias, gain, weight):
    return pl.pallas_call(
        project_kernel,
        in_specs=[WHOLE] * 6,
        out_specs=WHOLE,
        out_shape=jax.ShapeDtypeStruct((rows.shape[0], WIDTH), BF16),
        compiler_params=pltpu.CompilerParams(vmem_limit_bytes=16 * MIB),
        cost_estimate=pl.CostEstimate(
            flops=2 * rows.size * WIDTH, bytes_accessed=4 * MIB, transcendentals=0
        ),
        name="projection",
    )(rows, part_a, part_b, bias, gain, weight)


def handoff_kernel(seq_ref, pos_ref, own_ref, own_a, own_b, bias_ref, gain_ref, weight_ref,
                   peer_ref, out_ref):
    tokens = pos_ref.shape[1]
    own = project(own_ref, own_a, own_b, bias_ref, gain_ref, weight_ref)
    projected = jnp.concatenate([own, peer_ref[...]], axis=0)
    pos = pos_ref[...]
    chosen = ((pos >> 10) & 1) == seq_ref[0]
    clip_row = jnp.where(chosen, pos >> 11, -1).astype(F32)
    label_row = ((pos & (SPAN - 1)) + 1).astype(F32)
    down, across = iota((tokens, tokens), 0), iota((tokens, tokens), 1)
    same = down == across
    clip_col = jnp.sum(jnp.where(same, clip_row, 0.0), axis=1, keepdims=True)
    label_col = jnp.sum(jnp.where(same, label_row, 0.0), axis=1, keepdims=True)
    alike = clip_col == clip_row
    rank_col = jnp.sum(jnp.where(alike & (across < down), 1.0, 0.0), axis=1, keepdims=True)
    rank_row = jnp.sum(jnp.where(alike & (down < across), 1.0, 0.0), axis=0, keepdims=True)
    clips = out_ref.shape[0] // GROUP
    slot_row = jnp.where(clip_row >= 0, clip_row * GROUP + rank_row, -1.0).astype(jnp.int32)
    pick = (iota((clips * GROUP, tokens), 0) == slot_row).astype(F32).astype(BF16)
    packed = dot(pick, projected).astype(BF16).reshape(clips, GROUP, WIDTH)
    to_clip = (iota((clips, tokens), 0) == clip_row.astype(jnp.int32)).astype(F32).astype(BF16)
    upper = jnp.floor(label_col * (1.0 / 32.0))
    lower = label_col - 32.0 * upper
    lane = iota((tokens, 128), 1).astype(F32)
    codes = jnp.where(lane == rank_col, upper, 0.0) + jnp.where(lane == rank_col + 16.0, lower, 0.0)
    labels = dot(to_clip, codes.astype(BF16))
    first = jnp.where(
        iota((clips, GROUP, 128), 1) == LABEL_ROW,
        labels.reshape(clips, 1, 128),
        packed[:, :, :128].astype(F32),
    ).astype(BF16)
    out_ref[:, :128] = first.reshape(clips * GROUP, 128)
    out_ref[:, 128:] = packed[:, :, 128:].reshape(clips * GROUP, WIDTH - 128)


def handoff(seq, pos, own, own_a, own_b, bias, gain, weight, peer, clips):
    return pl.pallas_call(
        handoff_kernel,
        in_specs=[pl.BlockSpec(memory_space=pltpu.SMEM)] + [WHOLE] * 8,
        out_specs=WHOLE,
        out_shape=jax.ShapeDtypeStruct((clips * GROUP, WIDTH), BF16),
        compiler_params=pltpu.CompilerParams(vmem_limit_bytes=24 * MIB),
        cost_estimate=pl.CostEstimate(
            flops=2 * 512 * (704 * 512 + 1024 * 512), bytes_accessed=7 * MIB, transcendentals=0
        ),
        name="handoff",
    )(seq, pos, own, own_a, own_b, bias, gain, weight, peer)


def slot_labels(got_ref):
    slots = got_ref.shape[0]
    clips = slots // GROUP
    head = got_ref[:, :128].astype(F32).reshape(clips, GROUP, 128)
    codes = jnp.sum(jnp.where(iota(head.shape, 1) == LABEL_ROW, head, 0.0), axis=1)
    lane, place = iota((128, slots), 0), iota((128, slots), 1) % GROUP
    spread = jnp.where(lane == place, 32.0, 0.0) + jnp.where(lane == place + 16, 1.0, 0.0)
    by_clip = dot(codes.astype(BF16), spread.astype(BF16))
    mine = iota((clips, slots), 0) == iota((clips, slots), 1) // GROUP
    return jnp.sum(jnp.where(mine, by_clip, 0.0), axis=0, keepdims=True)


def stream_tile(half, first, count, got_ref, label_row, mask, parts):
    slots = got_ref.shape[0]
    want = (iota((count, slots), 0) + (first + 1)).astype(F32)
    place = (want == label_row).astype(F32)
    seen = jnp.sum(place, axis=1, keepdims=True)
    placed = dot(place.astype(BF16), got_ref[...])
    sin_a, cos_a, sin_b, cos_b = parts
    blocks = count // 32
    start = pl.multiple_of(half * (SPAN // 32) + first // 32, 8)
    coarse_sin = sin_a[pl.ds(start, blocks), :].reshape(blocks, 1, WIDTH)
    coarse_cos = cos_a[pl.ds(start, blocks), :].reshape(blocks, 1, WIDTH)
    table = coarse_sin * cos_b[...][None] + coarse_cos * sin_b[...][None]
    return placed + (1.0 - seen) * mask + table.reshape(count, WIDTH)


QKV_TILE = 512


def qkv_kernel(seq_ref, got_ref, sin_a, cos_a, sin_b, cos_b, mask_ref, gain_ref, weight_ref,
               bias_ref, stream_ref, query_ref, key_ref, value_ref):
    label_row = slot_labels(got_ref)
    scale = HEAD_D ** (-0.5) * math.log2(math.e)
    for first in range(0, SPAN, QKV_TILE):
        rows = pl.ds(first, QKV_TILE)
        stream = stream_tile(
            seq_ref[0], first, QKV_TILE, got_ref, label_row, mask_ref[...],
            (sin_a, cos_a, sin_b, cos_b),
        )
        stream_ref[rows, :] = stream
        normed = norm(stream, gain_ref[0:1, :]).astype(BF16)
        out = dot(normed, weight_ref[...]) + bias_ref[...]
        query_ref[rows, :] = (out[:, :WIDTH] * scale).astype(BF16)
        key_ref[rows, :] = out[:, WIDTH : 2 * WIDTH].astype(BF16)
        value_ref[:, rows] = out[:, 2 * WIDTH :].T.astype(BF16)


def own_qkv(seq, got, parts, mask, gain, weight, bias):
    return pl.pallas_call(
        qkv_kernel,
        in_specs=[pl.BlockSpec(memory_space=pltpu.SMEM)] + [WHOLE] * 9,
        out_specs=[WHOLE] * 4,
        out_shape=[
            jax.ShapeDtypeStruct((SPAN, WIDTH), F32),
            jax.ShapeDtypeStruct((SPAN, WIDTH), BF16),
            jax.ShapeDtypeStruct((SPAN, WIDTH), BF16),
            jax.ShapeDtypeStruct((WIDTH, SPAN), BF16),
        ],
        compiler_params=pltpu.CompilerParams(vmem_limit_bytes=20 * MIB),
        cost_estimate=pl.CostEstimate(
            flops=2 * SPAN * WIDTH * (3 * WIDTH + SPAN), bytes_accessed=9 * MIB, transcendentals=0
        ),
        name="own_qkv",
    )(seq, got, *parts, mask, gain, weight, bias)


ROW_TILE = 1024
FF_TILE = 512


def top(ref):
    head_of = (iota((WIDTH, 128), 0) // HEAD_D == iota((WIDTH, 128), 1)).astype(F32).astype(BF16)
    return jnp.max(dot(ref[...] * ref[...], head_of), axis=0, keepdims=True)


def is_safe(query_top, key_ref, value_ref):
    score_top = jnp.max(query_top * top(key_ref))
    value_top = jnp.max(jnp.abs(value_ref[...].astype(F32)))
    return (score_top <= SAFE * SAFE) & (value_top <= SAFE_VALUE)


def head_scores(query_ref, key_ref, pair, half):
    lanes = pl.ds(pl.multiple_of(pair * 128, 128), 128)
    query = query_ref[:, lanes]
    own_lane = (iota((1, 128), 1) < HEAD_D) == (half == 0)
    masked = jnp.where(own_lane, query, jnp.zeros_like(query))
    return lax.dot_general(
        key_ref[:, lanes], masked, (((1,), (1,)), ((), ())), preferred_element_type=F32
    )


def head_total(value_ref, weights, pair, half):
    value = value_ref[pl.ds(pl.multiple_of(pair * 128, 128), 128), :]
    own_row = (iota((128, 1), 0) < HEAD_D) == (half == 0)
    return dot(jnp.where(own_row, value, jnp.ones_like(value)), weights.astype(BF16))


def for_all_pairs(safe, attend):
    def run(peaked):
        def one_pair(pair, carry):
            attend(pair, peaked)
            return carry

        lax.fori_loop(0, HEADS // 2, one_pair, 0, unroll=1)

    pl.when(safe)(lambda: run(False))
    pl.when(jnp.logical_not(safe))(lambda: run(True))


def own_attention_kernel(query_ref, key_ref, value_ref, total_ref, shift_ref, top_ref, safe_ref):
    query_top = top(query_ref)
    top_ref[...] = query_top
    safe = is_safe(query_top, key_ref, value_ref)
    safe_ref[0] = safe.astype(jnp.int32)

    def attend(pair, peaked):
        for half in range(2):
            head = 2 * pair + half
            scores = head_scores(query_ref, key_ref, pair, half)
            if peaked:
                peak = jnp.max(scores, axis=0, keepdims=True)
                scores = scores - peak
                shift_ref[head] = peak
            else:
                shift_ref[head] = jnp.zeros((1, SPAN), F32)
            total_ref[head] = head_total(value_ref, jnp.exp2(scores), pair, half)

    for_all_pairs(safe, attend)


def own_attention(query, key, value):
    return pl.pallas_call(
        own_attention_kernel,
        in_specs=[WHOLE] * 3,
        out_specs=[WHOLE] * 3 + [pl.BlockSpec(memory_space=pltpu.SMEM)],
        out_shape=[
            jax.ShapeDtypeStruct((HEADS, 128, SPAN), F32),
            jax.ShapeDtypeStruct((HEADS, 1, SPAN), F32),
            jax.ShapeDtypeStruct((1, 128), F32),
            jax.ShapeDtypeStruct((1,), jnp.int32),
        ],
        compiler_params=pltpu.CompilerParams(vmem_limit_bytes=OWN_VMEM * MIB),
        cost_estimate=pl.CostEstimate(
            flops=16 * SPAN * SPAN * WIDTH,
            bytes_accessed=8 * MIB,
            transcendentals=HEADS * SPAN * SPAN,
        ),
        name="own_attention",
    )(query, key, value)


def decoder_kernel(safe_ref, query_ref, key_ref, value_ref, total_ref, shift_ref, top_ref,
                   stream_ref, gain_ref, out_weight_ref, out_bias_ref, fc1_ref, fc1_bias_ref,
                   fc2_ref, fc2_bias_ref, out_ref, attended, hidden):
    safe = (safe_ref[0] == 1) & is_safe(top_ref[...], key_ref, value_ref)

    def attend(pair, peaked):
        mixed = []
        for half in range(2):
            head = 2 * pair + half
            scores = head_scores(query_ref, key_ref, pair, half)
            before = total_ref[head]
            if peaked:
                shift = shift_ref[head]
                peak = jnp.maximum(shift, jnp.max(scores, axis=0, keepdims=True))
                scores = scores - peak
                before = before * jnp.exp2(shift - peak)
            mixed.append(before + head_total(value_ref, jnp.exp2(scores), pair, half))
        first = mixed[0][:HEAD_D] / mixed[0][HEAD_D:]
        second = mixed[1][HEAD_D:] / mixed[1][:HEAD_D]
        lanes = pl.ds(pl.multiple_of(pair * 128, 128), 128)
        attended[:, lanes] = jnp.concatenate([first, second], axis=0).T.astype(BF16)

    for_all_pairs(safe, attend)

    for first in range(0, SPAN, ROW_TILE):
        rows = pl.ds(first, ROW_TILE)
        stream2 = stream_ref[rows, :] + dot(attended[rows, :], out_weight_ref[...]) + out_bias_ref[...]
        normed2 = norm(stream2, gain_ref[1:2, :]).astype(BF16)
        for at in range(0, hidden.shape[1], FF_TILE):
            units = pl.ds(at, FF_TILE)
            inner = dot(normed2, fc1_ref[:, units]) + fc1_bias_ref[:, units]
            hidden[:, units] = gelu(inner).astype(BF16)
        out_ref[rows, :] = (stream2 + dot(hidden[...], fc2_ref[...]) + fc2_bias_ref[...]).astype(BF16)


def decoder(safe, *rest):
    fc1 = rest[-4]
    return pl.pallas_call(
        decoder_kernel,
        in_specs=[pl.BlockSpec(memory_space=pltpu.SMEM)] + [WHOLE] * len(rest),
        out_specs=WHOLE,
        out_shape=jax.ShapeDtypeStruct((SPAN, WIDTH), BF16),
        scratch_shapes=[
            pltpu.VMEM((SPAN, WIDTH), BF16),
            pltpu.VMEM((ROW_TILE, fc1.shape[1]), BF16),
        ],
        compiler_params=pltpu.CompilerParams(vmem_limit_bytes=DEC_VMEM * MIB),
        cost_estimate=pl.CostEstimate(
            flops=16 * SPAN * SPAN * WIDTH + 2 * SPAN * WIDTH * (WIDTH + 4096),
            bytes_accessed=16 * MIB,
            transcendentals=HEADS * SPAN * SPAN,
        ),
        name="decoder",
    )(safe, *rest)


OWN_VMEM = 18
DEC_VMEM = 24


def body(
    enc_rows,
    visible_pos,
    enc_norm_gain,
    enc_fc1,
    enc_fc1_bias,
    enc_fc2,
    enc_fc2_bias,
    handoff_weight,
    mask_token,
    dec_norm_gain,
    qkv_weight,
    qkv_bias,
    out_weight,
    out_bias,
    dec_fc1,
    dec_fc1_bias,
    dec_fc2,
    dec_fc2_bias,
):
    def swap(values):
        return lax.ppermute(values, "seq", [(0, 1), (1, 0)])

    def row(values):
        return values.reshape(1, -1)

    clips = lax.axis_size("rows")
    seq = lax.axis_index("seq").astype(jnp.int32).reshape(1)
    parts = tuple(jnp.asarray(part) for part in sinusoid_parts())
    bias1, bias2 = row(enc_fc1_bias), row(enc_fc2_bias)
    peer_rows = swap(enc_rows)
    peer_pos = swap(visible_pos)
    own_part, fc1_here, fc2_here = first_encoder_mlp(enc_rows, enc_norm_gain, enc_fc1, bias1, enc_fc2)
    peer_rows, peer_pos, own_part = lax.optimization_barrier((peer_rows, peer_pos, own_part))
    peer_part = second_encoder_mlp(peer_rows, enc_norm_gain, fc1_here, bias1, fc2_here)
    pos = jnp.concatenate([visible_pos, peer_pos]).reshape(1, -1)
    peer = projection(peer_rows, peer_part, swap(own_part), bias2, enc_norm_gain, handoff_weight)
    payload = handoff(
        seq, pos, enc_rows, own_part, swap(peer_part), bias2, enc_norm_gain, handoff_weight, peer, clips
    )
    mask, qkv_bias = row(mask_token), row(qkv_bias)
    payload, mask, qkv_bias = lax.optimization_barrier((payload, mask, qkv_bias))
    got = lax.all_to_all(
        payload.reshape(clips, GROUP, WIDTH), "rows", split_axis=0, concat_axis=0, tiled=True
    ).reshape(clips * GROUP, WIDTH)
    stream, query, key, value = own_qkv(
        seq, got, parts, mask, dec_norm_gain, qkv_weight, qkv_bias
    )
    peer_key, peer_value = swap(key), swap(value)
    total, shift, query_top, safe = own_attention(query, key, value)
    decoded = decoder(
        safe, query, peer_key, peer_value, total, shift, query_top, stream, dec_norm_gain,
        out_weight, row(out_bias), dec_fc1, row(dec_fc1_bias), dec_fc2, row(dec_fc2_bias),
    )
    return decoded.reshape(1, SPAN, WIDTH)


def solution(mesh):
    return jax.shard_map(
        body,
        mesh=mesh,
        in_specs=(
            P(("rows", "seq"), None),
            P(("rows", "seq")),
            P(),
            P(None, "seq"),
            P("seq"),
            P("seq", None),
            P(),
            P(),
            P(),
            P(),
            P(),
            P(),
            P(),
            P(),
            P(),
            P(),
            P(),
            P(),
        ),
        out_specs=P("rows", "seq", None),
        check_vma=False,
    )
```

```python
import math

import jax
import jax.numpy as jnp
import numpy as np
from jax import lax
from jax.experimental import pallas as pl
from jax.experimental.pallas import tpu as pltpu
from jax.sharding import PartitionSpec as P

HEADS = 8
CLIP_LEN = 2048
SPAN = 1024
WIDTH = 512
HEAD_D = 64
GROUP = 16
LABEL_ROW = 12
EPS = 1e-06
F32 = jnp.float32
BF16 = jnp.bfloat16
MIB = 1 << 20
WHOLE = pl.BlockSpec(memory_space=pltpu.VMEM)
SAFE = 60.0
SAFE_VALUE = 2.0**40

def norm(values, gain):
    mean = jnp.mean(values, axis=-1, keepdims=True)
    centered = values - mean
    spread = jnp.mean(centered * centered, axis=-1, keepdims=True)
    return centered * lax.rsqrt(spread + EPS) * gain


def gelu(x):
    half = 0.5 * x
    return half + half * lax.erf(x * (0.5**0.5))


def dot(a, b):
    return jnp.dot(a, b, preferred_element_type=F32)


def iota(shape, dim):
    return lax.broadcasted_iota(jnp.int32, shape, dim)


def sinusoid_parts():
    column = np.arange(WIDTH)
    rate = 10000.0 ** (-(2 * (column // 2)) / WIDTH)
    phase = np.where(column % 2 == 0, 0.0, np.pi / 2)
    coarse = 32.0 * np.arange(CLIP_LEN // 32)[:, None] * rate[None, :] + phase[None, :]
    fine = np.arange(32)[:, None] * rate[None, :]
    return tuple(
        np.asarray(part, np.float32)
        for part in (np.sin(coarse), np.cos(coarse), np.sin(fine), np.cos(fine))
    )


ENC_TILE = 512
IN_FLIGHT = 2
IN_SIZES = (1024, 2048)
OUT_SIZES = (1408,)


def tiles_of(sizes):
    starts = [sum(sizes[:i]) for i in range(len(sizes))]
    return [(start, start + size) for start, size in zip(starts, sizes)]


def cut(start, stop):
    return [pl.ds(at, min(ENC_TILE, stop - at)) for at in range(start, stop, ENC_TILE)]


def enc_kernel(rows_ref, gain_ref, w1_ref, b1_ref, w2_ref, out_ref, w1, w2, rows, gain, b1, hidden,
               arrived, arrived1, arrived2):
    small = [
        pltpu.make_async_copy(source, target, arrived.at[i])
        for i, (source, target) in enumerate(((rows_ref, rows), (gain_ref, gain), (b1_ref, b1)))
    ]
    loads = []
    for sizes, source, target, sems in ((IN_SIZES, w1_ref, w1, arrived1), (OUT_SIZES, w2_ref, w2, arrived2)):
        for i, (start, stop) in enumerate(tiles_of(sizes)):
            tile = pl.ds(start, stop - start)
            loads.append(pltpu.make_async_copy(source.at[:, tile], target.at[:, tile], sems.at[i]))
    for load in small + loads[:IN_FLIGHT]:
        load.start()

    def take(i):
        loads[i].wait()
        if i + IN_FLIGHT < len(loads):
            loads[i + IN_FLIGHT].start()

    for load in small:
        load.wait()
    normed = norm(rows[...].astype(F32), gain[0:1, :]).astype(BF16)
    for i, (start, stop) in enumerate(tiles_of(IN_SIZES)):
        take(i)
        for tile in cut(start, stop):
            hidden[:, tile] = gelu(dot(normed, w1[:, tile]) + b1[:, tile]).astype(BF16)
    for i, (start, stop) in enumerate(tiles_of(OUT_SIZES)):
        take(len(IN_SIZES) + i)
        for tile in cut(start, stop):
            out_ref[:, tile] = dot(hidden[...], w2[:, tile]).astype(BF16)


def enc_cost(count, width, units):
    return pl.CostEstimate(
        flops=4 * count * width * units,
        bytes_accessed=4 * width * units + 4 * count * width,
        transcendentals=count * units,
    )


def first_encoder_mlp(rows, gain, w1, b1, w2):
    count, width = rows.shape
    units = w1.shape[1]
    far = pl.BlockSpec(memory_space=pl.ANY)
    return pl.pallas_call(
        enc_kernel,
        in_specs=[far] * 5,
        out_specs=[WHOLE] * 3,
        out_shape=[
            jax.ShapeDtypeStruct((count, width), BF16),
            jax.ShapeDtypeStruct(w1.shape, BF16),
            jax.ShapeDtypeStruct(w2.shape, BF16),
        ],
        scratch_shapes=[
            pltpu.VMEM((count, width), BF16),
            pltpu.VMEM(gain.shape, F32),
            pltpu.VMEM(b1.shape, F32),
            pltpu.VMEM((count, units), BF16),
            pltpu.SemaphoreType.DMA((3,)),
            pltpu.SemaphoreType.DMA((len(IN_SIZES),)),
            pltpu.SemaphoreType.DMA((len(OUT_SIZES),)),
        ],
        compiler_params=pltpu.CompilerParams(vmem_limit_bytes=FIRST_VMEM),
        cost_estimate=enc_cost(count, width, units),
        name="first_encoder_mlp",
    )(rows, gain, w1, b1, w2)


def second_enc_kernel(rows_ref, gain_ref, w1, b1, w2, out_ref, hidden):
    units, width = w2.shape
    normed = norm(rows_ref[...].astype(F32), gain_ref[0:1, :]).astype(BF16)
    for tile in cut(0, units):
        hidden[:, tile] = gelu(dot(normed, w1[:, tile]) + b1[:, tile]).astype(BF16)
    for tile in cut(0, width):
        out_ref[:, tile] = dot(hidden[...], w2[:, tile]).astype(BF16)


def second_encoder_mlp(rows, gain, w1, b1, w2):
    count, width = rows.shape
    units = w1.shape[1]
    return pl.pallas_call(
        second_enc_kernel,
        in_specs=[WHOLE] * 5,
        out_specs=WHOLE,
        out_shape=jax.ShapeDtypeStruct((count, width), BF16),
        scratch_shapes=[pltpu.VMEM((count, units), BF16)],
        compiler_params=pltpu.CompilerParams(vmem_limit_bytes=ENC_VMEM * MIB),
        cost_estimate=enc_cost(count, width, units),
        name="second_encoder_mlp",
    )(rows, gain, w1, b1, w2)
ENC_VMEM = 16
FIRST_VMEM = 34 * MIB


def project(rows, part_a, part_b, bias_ref, gain_ref, weight_ref):
    encoded = (
        rows[...].astype(F32) + (part_a[...].astype(F32) + part_b[...].astype(F32)) + bias_ref[...]
    )
    final = norm(encoded, gain_ref[1:2, :]).astype(BF16)
    return dot(final, weight_ref[...]).astype(BF16)


def project_kernel(rows, part_a, part_b, bias_ref, gain_ref, weight_ref, out_ref):
    out_ref[...] = project(rows, part_a, part_b, bias_ref, gain_ref, weight_ref)


def projection(rows, part_a, part_b, bias, gain, weight):
    return pl.pallas_call(
        project_kernel,
        in_specs=[WHOLE] * 6,
        out_specs=WHOLE,
        out_shape=jax.ShapeDtypeStruct((rows.shape[0], WIDTH), BF16),
        compiler_params=pltpu.CompilerParams(vmem_limit_bytes=16 * MIB),
        cost_estimate=pl.CostEstimate(
            flops=2 * rows.size * WIDTH, bytes_accessed=4 * MIB, transcendentals=0
        ),
        name="projection",
    )(rows, part_a, part_b, bias, gain, weight)


def handoff_kernel(seq_ref, pos_ref, own_ref, own_a, own_b, bias_ref, gain_ref, weight_ref,
                   peer_ref, out_ref):
    tokens = pos_ref.shape[1]
    own = project(own_ref, own_a, own_b, bias_ref, gain_ref, weight_ref)
    projected = jnp.concatenate([own, peer_ref[...]], axis=0)
    pos = pos_ref[...]
    chosen = ((pos >> 10) & 1) == seq_ref[0]
    clip_row = jnp.where(chosen, pos >> 11, -1).astype(F32)
    label_row = ((pos & (SPAN - 1)) + 1).astype(F32)
    down, across = iota((tokens, tokens), 0), iota((tokens, tokens), 1)
    same = down == across
    clip_col = jnp.sum(jnp.where(same, clip_row, 0.0), axis=1, keepdims=True)
    label_col = jnp.sum(jnp.where(same, label_row, 0.0), axis=1, keepdims=True)
    alike = clip_col == clip_row
    rank_col = jnp.sum(jnp.where(alike & (across < down), 1.0, 0.0), axis=1, keepdims=True)
    rank_row = jnp.sum(jnp.where(alike & (down < across), 1.0, 0.0), axis=0, keepdims=True)
    clips = out_ref.shape[0] // GROUP
    slot_row = jnp.where(clip_row >= 0, clip_row * GROUP + rank_row, -1.0).astype(jnp.int32)
    pick = (iota((clips * GROUP, tokens), 0) == slot_row).astype(F32).astype(BF16)
    packed = dot(pick, projected).astype(BF16).reshape(clips, GROUP, WIDTH)
    to_clip = (iota((clips, tokens), 0) == clip_row.astype(jnp.int32)).astype(F32).astype(BF16)
    upper = jnp.floor(label_col * (1.0 / 32.0))
    lower = label_col - 32.0 * upper
    lane = iota((tokens, 128), 1).astype(F32)
    codes = jnp.where(lane == rank_col, upper, 0.0) + jnp.where(lane == rank_col + 16.0, lower, 0.0)
    labels = dot(to_clip, codes.astype(BF16))
    first = jnp.where(
        iota((clips, GROUP, 128), 1) == LABEL_ROW,
        labels.reshape(clips, 1, 128),
        packed[:, :, :128].astype(F32),
    ).astype(BF16)
    out_ref[:, :128] = first.reshape(clips * GROUP, 128)
    out_ref[:, 128:] = packed[:, :, 128:].reshape(clips * GROUP, WIDTH - 128)


def handoff(seq, pos, own, own_a, own_b, bias, gain, weight, peer, clips):
    return pl.pallas_call(
        handoff_kernel,
        in_specs=[pl.BlockSpec(memory_space=pltpu.SMEM)] + [WHOLE] * 8,
        out_specs=WHOLE,
        out_shape=jax.ShapeDtypeStruct((clips * GROUP, WIDTH), BF16),
        compiler_params=pltpu.CompilerParams(vmem_limit_bytes=24 * MIB),
        cost_estimate=pl.CostEstimate(
            flops=2 * 512 * (704 * 512 + 1024 * 512), bytes_accessed=7 * MIB, transcendentals=0
        ),
        name="handoff",
    )(seq, pos, own, own_a, own_b, bias, gain, weight, peer)


def slot_labels(got_ref):
    slots = got_ref.shape[0]
    clips = slots // GROUP
    head = got_ref[:, :128].astype(F32).reshape(clips, GROUP, 128)
    codes = jnp.sum(jnp.where(iota(head.shape, 1) == LABEL_ROW, head, 0.0), axis=1)
    lane, place = iota((128, slots), 0), iota((128, slots), 1) % GROUP
    spread = jnp.where(lane == place, 32.0, 0.0) + jnp.where(lane == place + 16, 1.0, 0.0)
    by_clip = dot(codes.astype(BF16), spread.astype(BF16))
    mine = iota((clips, slots), 0) == iota((clips, slots), 1) // GROUP
    return jnp.sum(jnp.where(mine, by_clip, 0.0), axis=0, keepdims=True)


def stream_tile(half, first, count, got_ref, label_row, mask, parts):
    slots = got_ref.shape[0]
    want = (iota((count, slots), 0) + (first + 1)).astype(F32)
    place = (want == label_row).astype(F32)
    seen = jnp.sum(place, axis=1, keepdims=True)
    placed = dot(place.astype(BF16), got_ref[...])
    sin_a, cos_a, sin_b, cos_b = parts
    blocks = count // 32
    start = pl.multiple_of(half * (SPAN // 32) + first // 32, 8)
    coarse_sin = sin_a[pl.ds(start, blocks), :].reshape(blocks, 1, WIDTH)
    coarse_cos = cos_a[pl.ds(start, blocks), :].reshape(blocks, 1, WIDTH)
    table = coarse_sin * cos_b[...][None] + coarse_cos * sin_b[...][None]
    return placed + (1.0 - seen) * mask + table.reshape(count, WIDTH)


QKV_TILE = 512


def qkv_kernel(seq_ref, got_ref, sin_a, cos_a, sin_b, cos_b, mask_ref, gain_ref, weight_ref,
               bias_ref, stream_ref, query_ref, key_ref, value_ref):
    label_row = slot_labels(got_ref)
    scale = HEAD_D ** (-0.5) * math.log2(math.e)
    for first in range(0, SPAN, QKV_TILE):
        rows = pl.ds(first, QKV_TILE)
        stream = stream_tile(
            seq_ref[0], first, QKV_TILE, got_ref, label_row, mask_ref[...],
            (sin_a, cos_a, sin_b, cos_b),
        )
        stream_ref[rows, :] = stream
        normed = norm(stream, gain_ref[0:1, :]).astype(BF16)
        out = dot(normed, weight_ref[...]) + bias_ref[...]
        query_ref[rows, :] = (out[:, :WIDTH] * scale).astype(BF16)
        key_ref[rows, :] = out[:, WIDTH : 2 * WIDTH].astype(BF16)
        value_ref[:, rows] = out[:, 2 * WIDTH :].T.astype(BF16)


def own_qkv(seq, got, parts, mask, gain, weight, bias):
    return pl.pallas_call(
        qkv_kernel,
        in_specs=[pl.BlockSpec(memory_space=pltpu.SMEM)] + [WHOLE] * 9,
        out_specs=[WHOLE] * 4,
        out_shape=[
            jax.ShapeDtypeStruct((SPAN, WIDTH), F32),
            jax.ShapeDtypeStruct((SPAN, WIDTH), BF16),
            jax.ShapeDtypeStruct((SPAN, WIDTH), BF16),
            jax.ShapeDtypeStruct((WIDTH, SPAN), BF16),
        ],
        compiler_params=pltpu.CompilerParams(vmem_limit_bytes=20 * MIB),
        cost_estimate=pl.CostEstimate(
            flops=2 * SPAN * WIDTH * (3 * WIDTH + SPAN), bytes_accessed=9 * MIB, transcendentals=0
        ),
        name="own_qkv",
    )(seq, got, *parts, mask, gain, weight, bias)


ROW_TILE = 1024
FF_TILE = 512


def top(ref):
    head_of = (iota((WIDTH, 128), 0) // HEAD_D == iota((WIDTH, 128), 1)).astype(F32).astype(BF16)
    return jnp.max(dot(ref[...] * ref[...], head_of), axis=0, keepdims=True)


def is_safe(query_top, key_ref, value_ref):
    score_top = jnp.max(query_top * top(key_ref))
    sizes = jnp.abs(value_ref[...])
    while sizes.shape[0] > 16:
        middle = sizes.shape[0] // 2
        sizes = jnp.maximum(sizes[:middle], sizes[middle:])
    value_top = jnp.max(sizes.astype(F32))
    return (score_top <= SAFE * SAFE) & (value_top <= SAFE_VALUE)


def head_scores(query_ref, key_ref, pair, half):
    lanes = pl.ds(pl.multiple_of(pair * 128, 128), 128)
    query = query_ref[:, lanes]
    own_lane = (iota((1, 128), 1) < HEAD_D) == (half == 0)
    masked = jnp.where(own_lane, query, jnp.zeros_like(query))
    return lax.dot_general(
        key_ref[:, lanes], masked, (((1,), (1,)), ((), ())), preferred_element_type=F32
    )


def head_total(value_ref, weights, pair, half):
    value = value_ref[pl.ds(pl.multiple_of(pair * 128, 128), 128), :]
    own_row = (iota((128, 1), 0) < HEAD_D) == (half == 0)
    return dot(jnp.where(own_row, value, jnp.ones_like(value)), weights.astype(BF16))


def for_all_pairs(safe, attend):
    def run(peaked):
        def one_pair(pair, carry):
            attend(pair, peaked)
            return carry

        lax.fori_loop(0, HEADS // 2, one_pair, 0, unroll=1)

    pl.when(safe)(lambda: run(False))
    pl.when(jnp.logical_not(safe))(lambda: run(True))


def own_attention_kernel(query_ref, key_ref, value_ref, total_ref, shift_ref, top_ref, safe_ref):
    query_top = top(query_ref)
    top_ref[...] = query_top
    safe = is_safe(query_top, key_ref, value_ref)
    safe_ref[0] = safe.astype(jnp.int32)

    def attend(pair, peaked):
        for half in range(2):
            head = 2 * pair + half
            scores = head_scores(query_ref, key_ref, pair, half)
            if peaked:
                peak = jnp.max(scores, axis=0, keepdims=True)
                scores = scores - peak
                shift_ref[head] = peak
            else:
                shift_ref[head] = jnp.zeros((1, SPAN), F32)
            total_ref[head] = head_total(value_ref, jnp.exp2(scores), pair, half)

    for_all_pairs(safe, attend)


def own_attention(query, key, value):
    return pl.pallas_call(
        own_attention_kernel,
        in_specs=[WHOLE] * 3,
        out_specs=[WHOLE] * 3 + [pl.BlockSpec(memory_space=pltpu.SMEM)],
        out_shape=[
            jax.ShapeDtypeStruct((HEADS, 128, SPAN), F32),
            jax.ShapeDtypeStruct((HEADS, 1, SPAN), F32),
            jax.ShapeDtypeStruct((1, 128), F32),
            jax.ShapeDtypeStruct((1,), jnp.int32),
        ],
        compiler_params=pltpu.CompilerParams(vmem_limit_bytes=OWN_VMEM * MIB),
        cost_estimate=pl.CostEstimate(
            flops=16 * SPAN * SPAN * WIDTH,
            bytes_accessed=8 * MIB,
            transcendentals=HEADS * SPAN * SPAN,
        ),
        name="own_attention",
    )(query, key, value)


def decoder_kernel(safe_ref, query_ref, key_ref, value_ref, total_ref, shift_ref, top_ref,
                   stream_ref, gain_ref, out_weight_ref, out_bias_ref, fc1_ref, fc1_bias_ref,
                   fc2_ref, fc2_bias_ref, out_ref, attended, hidden):
    safe = (safe_ref[0] == 1) & is_safe(top_ref[...], key_ref, value_ref)

    def attend(pair, peaked):
        mixed = []
        for half in range(2):
            head = 2 * pair + half
            scores = head_scores(query_ref, key_ref, pair, half)
            before = total_ref[head]
            if peaked:
                shift = shift_ref[head]
                peak = jnp.maximum(shift, jnp.max(scores, axis=0, keepdims=True))
                scores = scores - peak
                before = before * jnp.exp2(shift - peak)
            mixed.append(before + head_total(value_ref, jnp.exp2(scores), pair, half))
        first = mixed[0][:HEAD_D] / mixed[0][HEAD_D:]
        second = mixed[1][HEAD_D:] / mixed[1][:HEAD_D]
        lanes = pl.ds(pl.multiple_of(pair * 128, 128), 128)
        attended[:, lanes] = jnp.concatenate([first, second], axis=0).T.astype(BF16)

    for_all_pairs(safe, attend)

    for first in range(0, SPAN, ROW_TILE):
        rows = pl.ds(first, ROW_TILE)
        stream2 = stream_ref[rows, :] + dot(attended[rows, :], out_weight_ref[...]) + out_bias_ref[...]
        normed2 = norm(stream2, gain_ref[1:2, :]).astype(BF16)
        for at in range(0, hidden.shape[1], FF_TILE):
            units = pl.ds(at, FF_TILE)
            inner = dot(normed2, fc1_ref[:, units]) + fc1_bias_ref[:, units]
            hidden[:, units] = gelu(inner).astype(BF16)
        out_ref[rows, :] = (stream2 + dot(hidden[...], fc2_ref[...]) + fc2_bias_ref[...]).astype(BF16)


def decoder(safe, *rest):
    fc1 = rest[-4]
    return pl.pallas_call(
        decoder_kernel,
        in_specs=[pl.BlockSpec(memory_space=pltpu.SMEM)] + [WHOLE] * len(rest),
        out_specs=WHOLE,
        out_shape=jax.ShapeDtypeStruct((SPAN, WIDTH), BF16),
        scratch_shapes=[
            pltpu.VMEM((SPAN, WIDTH), BF16),
            pltpu.VMEM((ROW_TILE, fc1.shape[1]), BF16),
        ],
        compiler_params=pltpu.CompilerParams(vmem_limit_bytes=DEC_VMEM * MIB),
        cost_estimate=pl.CostEstimate(
            flops=16 * SPAN * SPAN * WIDTH + 2 * SPAN * WIDTH * (WIDTH + 4096),
            bytes_accessed=16 * MIB,
            transcendentals=HEADS * SPAN * SPAN,
        ),
        name="decoder",
    )(safe, *rest)


OWN_VMEM = 18
DEC_VMEM = 24


def body(
    enc_rows,
    visible_pos,
    enc_norm_gain,
    enc_fc1,
    enc_fc1_bias,
    enc_fc2,
    enc_fc2_bias,
    handoff_weight,
    mask_token,
    dec_norm_gain,
    qkv_weight,
    qkv_bias,
    out_weight,
    out_bias,
    dec_fc1,
    dec_fc1_bias,
    dec_fc2,
    dec_fc2_bias,
):
    def swap(values):
        return lax.ppermute(values, "seq", [(0, 1), (1, 0)])

    def row(values):
        return values.reshape(1, -1)

    clips = lax.axis_size("rows")
    seq = lax.axis_index("seq").astype(jnp.int32).reshape(1)
    parts = tuple(jnp.asarray(part) for part in sinusoid_parts())
    bias1, bias2 = row(enc_fc1_bias), row(enc_fc2_bias)
    peer_rows = swap(enc_rows)
    peer_pos = swap(visible_pos)
    own_part, fc1_here, fc2_here = first_encoder_mlp(enc_rows, enc_norm_gain, enc_fc1, bias1, enc_fc2)
    peer_rows, peer_pos, own_part = lax.optimization_barrier((peer_rows, peer_pos, own_part))
    peer_part = second_encoder_mlp(peer_rows, enc_norm_gain, fc1_here, bias1, fc2_here)
    pos = jnp.concatenate([visible_pos, peer_pos]).reshape(1, -1)
    peer = projection(peer_rows, peer_part, swap(own_part), bias2, enc_norm_gain, handoff_weight)
    payload = handoff(
        seq, pos, enc_rows, own_part, swap(peer_part), bias2, enc_norm_gain, handoff_weight, peer, clips
    )
    mask, qkv_bias = row(mask_token), row(qkv_bias)
    payload, mask, qkv_bias = lax.optimization_barrier((payload, mask, qkv_bias))
    got = lax.all_to_all(
        payload.reshape(clips, GROUP, WIDTH), "rows", split_axis=0, concat_axis=0, tiled=True
    ).reshape(clips * GROUP, WIDTH)
    stream, query, key, value = own_qkv(
        seq, got, parts, mask, dec_norm_gain, qkv_weight, qkv_bias
    )
    peer_key, peer_value = swap(key), swap(value)
    total, shift, query_top, safe = own_attention(query, key, value)
    decoded = decoder(
        safe, query, peer_key, peer_value, total, shift, query_top, stream, dec_norm_gain,
        out_weight, row(out_bias), dec_fc1, row(dec_fc1_bias), dec_fc2, row(dec_fc2_bias),
    )
    return decoded.reshape(1, SPAN, WIDTH)


def solution(mesh):
    return jax.shard_map(
        body,
        mesh=mesh,
        in_specs=(
            P(("rows", "seq"), None),
            P(("rows", "seq")),
            P(),
            P(None, "seq"),
            P("seq"),
            P("seq", None),
            P(),
            P(),
            P(),
            P(),
            P(),
            P(),
            P(),
            P(),
            P(),
            P(),
            P(),
            P(),
        ),
        out_specs=P("rows", "seq", None),
        check_vma=False,
    )
```
